256 devices in a mesh: dp: 256 (over z, y, x, core).
Axes of the slice: x: 4, y: 4, z: 8, core: 2. Of those that a mesh axis runs over, the one named last changes fastest.
Arguments:
- left_embed: float32 [18432, 384], P('dp'), may hold values from -6 to 6
- right_embed: float32 [18432, 384], P('dp'), may hold values from -6 to 6
Outputs:
- left_grad: float32 [18432, 384], P('dp')
- right_grad: float32 [18432, 384], P('dp')
- mean_loss: float32 [], replicated
The draws below stay inside these ranges and needn't reach their ends.
All inputs are finite; a program needn't handle non-finite values.
Results may differ from the reference program's by a relative error of at most 0.0056.
The reference program's roundings to bfloat16 on the way (of `left_bf`, `right_bf` and `weights_bf`) count: a program that leaves them out, or rounds other values in their place, can miss the bound.
Values may be sent and summed in bfloat16 or wider, within the bound.
A program may use at most 256 MiB of HBM per device.

```python
import math
import jax
import jax.numpy as jnp
from jax import lax

D = 384
ROWS_DEV = 72
PAIRS = 18432
N_DP = 256


def common_part(key):
    return jax.random.normal(jax.random.fold_in(key, 100), (PAIRS, D), jnp.float32)


def draw_left_embed(key, part):
    common = common_part(key)
    key = jax.random.fold_in(key, 1)
    result = 0.6 * common + 0.8 * jax.random.normal(jax.random.fold_in(key, 1), (PAIRS, D), jnp.float32)
    return jnp.clip(result, -6.0, 6.0)


def draw_right_embed(key, part):
    common = common_part(key)
    key = jax.random.fold_in(key, 2)
    result = 0.6 * common + 0.8 * jax.random.normal(jax.random.fold_in(key, 1), (PAIRS, D), jnp.float32)
    return jnp.clip(result, -6.0, 6.0)


def setup_inputs(seed: int = 0) -> dict:
    arg_keys = jax.random.split(jax.random.key(seed), 3)
    left_embed = draw_left_embed(jax.random.fold_in(arg_keys[2], 71), 0)
    right_embed = draw_right_embed(jax.random.fold_in(arg_keys[2], 71), 0)
    return {"left_embed": left_embed, "right_embed": right_embed}


def block_scores(left_rows, right_all):
    return lax.dot_general(left_rows, right_all, (((1,), (1,)), ((), ())), preferred_element_type=jnp.float32) * (2.0 / math.sqrt(D))

def reference(left_embed, right_embed):
    left_bf = left_embed.astype(jnp.bfloat16)
    right_bf = right_embed.astype(jnp.bfloat16)
    blocks = left_bf.reshape(N_DP, ROWS_DEV, D)

    def first_pass(running, left_rows):
        column_peak, column_mass = running
        scores = block_scores(left_rows, right_bf)
        row_peak = lax.optimization_barrier(jnp.max(scores, axis=1))
        row_lse = row_peak + jnp.log(lax.optimization_barrier(jnp.sum(jnp.exp(scores - row_peak[:, None]), axis=1)))
        new_peak = jnp.maximum(column_peak, lax.optimization_barrier(jnp.max(scores, axis=0)))
        new_mass = column_mass * jnp.exp(column_peak - new_peak) + lax.optimization_barrier(jnp.sum(jnp.exp(scores - new_peak[None, :]), axis=0))
        return ((new_peak, new_mass), row_lse)
    start_state = (jnp.full((PAIRS,), -1e+30, jnp.float32), jnp.zeros((PAIRS,), jnp.float32))
    (column_peak, column_mass), row_lse = lax.scan(first_pass, start_state, blocks)
    column_lse = column_peak + jnp.log(column_mass)
    matched = lax.optimization_barrier(jnp.sum(left_bf.astype(jnp.float32) * right_bf.astype(jnp.float32), axis=1)) * (2.0 / math.sqrt(D))
    mean_loss = jnp.sum(row_lse.reshape(PAIRS) + column_lse - 2.0 * matched) / (2.0 * PAIRS)
    columns = jnp.arange(PAIRS, dtype=jnp.int32)

    def second_pass(right_total, inputs):
        left_rows, block_lse, block_index = inputs
        scores = block_scores(left_rows, right_bf)
        here = block_index * ROWS_DEV + jnp.arange(ROWS_DEV, dtype=jnp.int32)
        weights = jnp.exp(scores - block_lse[:, None]) + jnp.exp(scores - column_lse[None, :])
        weights = jnp.where(columns[None, :] == here[:, None], weights - 2.0, weights)
        weights_bf = weights.astype(jnp.bfloat16)
        left_part = jnp.dot(weights_bf, right_bf, preferred_element_type=jnp.float32)
        right_total = right_total + lax.dot_general(weights_bf, left_rows, (((0,), (0,)), ((), ())), preferred_element_type=jnp.float32)
        return (right_total, left_part)
    right_grad, left_parts = lax.scan(second_pass, jnp.zeros((PAIRS, D), jnp.float32), (blocks, row_lse, jnp.arange(N_DP, dtype=jnp.int32)))
    return (left_parts.reshape(PAIRS, D), right_grad, mean_loss)
```

```python
import functools
import math

import jax
import jax.numpy as jnp
from jax import lax
from jax.experimental import pallas as pl
from jax.experimental.pallas import tpu as pltpu
from jax.sharding import PartitionSpec as P

MESH = pl.DeviceIdType.MESH
G = 16
ROWS = 72
D = 384
B = G * ROWS
TM = 288
T = B // TM
PER = TM // ROWS
LOG2E = math.log2(math.e)
LN2 = math.log(2.0)


def kernel(
    left_ref, right_ref, lgrad_ref, rgrad_ref, loss_ref,
    lg, rg, lall, rall, er, ec, w, rm_s, rl_s, cm_s, cs_s, rp,
    row_stat, col_stat, ls, rs, lr, rr, part, parts_a, parts_b,
    s_lg, r_lg, s_rg, r_rg, s_st, r_st, s_ls, r_ls, s_rs, r_rs, s_pa, r_pa, s_pb, r_pb,
):
    me = lax.axis_index("dp")
    core = me % 2
    p = (me // 2) % G
    z = me // (2 * G)
    q = z * 2 + core
    scale = 2.0 / math.sqrt(D) * LOG2E

    def plane_dev(k):
        return (z * (2 * G) + k * 2 + core,)

    def line_dev(k):
        return ((k // 2) * (2 * G) + p * 2 + k % 2,)

    barrier = pltpu.get_barrier_semaphore()

    @pl.loop(1, G)
    def _(m):
        pl.semaphore_signal(barrier, inc=1, device_id=plane_dev((p + m) % G), device_id_type=MESH)
        pl.semaphore_signal(barrier, inc=1, device_id=line_dev((q + m) % G), device_id_type=MESH)

    lbf = left_ref[...].astype(jnp.bfloat16)
    rbf = right_ref[...].astype(jnp.bfloat16)
    lg[p] = lbf
    rg[q] = rbf
    matched = jnp.sum(lbf.astype(jnp.float32) * rbf.astype(jnp.float32)) * scale
    pl.semaphore_wait(barrier, 2 * (G - 1))

    def copy(src, dst, send, recv, dev):
        return pltpu.make_async_remote_copy(
            src_ref=src, dst_ref=dst, send_sem=send, recv_sem=recv, device_id=dev, device_id_type=MESH
        )

    @pl.loop(1, G)
    def _(m):
        k = (p + m) % G
        copy(lg.at[p], lg.at[p], s_lg.at[k], r_lg.at[p], plane_dev(k)).start()
        k = (q + m) % G
        copy(rg.at[q], rg.at[q], s_rg.at[k], r_rg.at[q], line_dev(k)).start()

    @pl.loop(1, G)
    def _(m):
        k = (p + m) % G
        copy(lg.at[p], lg.at[k], s_lg.at[k], r_lg.at[k], plane_dev(k)).wait()
        k = (q + m) % G
        copy(rg.at[q], rg.at[k], s_rg.at[k], r_rg.at[k], line_dev(k)).wait()

    @pl.loop(0, G // 2)
    def _(j):
        at = pl.ds(pl.multiple_of(j * 2 * ROWS, 2 * ROWS), 2 * ROWS)
        for src, dst in ((lg, lall), (rg, rall)):
            two = [src[2 * j].astype(jnp.float32), src[2 * j + 1].astype(jnp.float32)]
            dst[at, :] = jnp.concatenate(two, axis=0).astype(jnp.bfloat16)

    @pl.loop(0, T)
    def _(t):
        at = pl.ds(pl.multiple_of(t * TM, TM), TM)
        s = lax.dot_general(
            lall[at, :], rall[...], (((1,), (1,)), ((), ())), preferred_element_type=jnp.float32
        ) * scale
        rm = jnp.max(s, axis=1, keepdims=True)
        e = jnp.exp2(s - rm)
        er[at, :] = e
        rm_s[at, :] = jnp.broadcast_to(rm, (TM, 128))
        rl_s[at, :] = jnp.broadcast_to(rm + jnp.log2(jnp.sum(e, axis=1, keepdims=True)), (TM, 128))
        cm = jnp.max(s, axis=0, keepdims=True)
        e = jnp.exp2(s - cm)
        ec[at, :] = e
        cm_s[t] = cm
        cs_s[t] = jnp.sum(e, axis=0, keepdims=True)

    cm = jnp.max(cm_s[...], axis=0)
    cs = jnp.sum(cs_s[...] * jnp.exp2(cm_s[...] - cm[None]), axis=0)
    col_stat[q] = cm + jnp.log2(cs)
    row_stat[p] = jnp.transpose(rl_s[...])[0:1, :]

    @pl.loop(1, G)
    def _(m):
        k = (p + m) % G
        copy(row_stat.at[p], row_stat.at[p], s_st.at[k], r_st.at[p], plane_dev(k)).start()
        k = (q + m) % G
        copy(col_stat.at[q], col_stat.at[q], s_st.at[G + k], r_st.at[G + q], line_dev(k)).start()

    @pl.loop(1, G)
    def _(m):
        k = (p + m) % G
        copy(row_stat.at[p], row_stat.at[k], s_st.at[k], r_st.at[k], plane_dev(k)).wait()
        k = (q + m) % G
        copy(col_stat.at[q], col_stat.at[k], s_st.at[G + k], r_st.at[G + k], line_dev(k)).wait()

    def combine(ref):
        v = ref[...]
        top = jnp.max(v, axis=0)
        return top + jnp.log2(jnp.sum(jnp.exp2(v - top[None]), axis=0))

    row_lse = combine(row_stat)
    col_lse = combine(col_stat)
    row_lse_col = jnp.transpose(jnp.broadcast_to(row_lse, (128, B)))
    rm_s[...] = jnp.exp2(rm_s[...] - row_lse_col)

    lane = lax.broadcasted_iota(jnp.int32, (1, B), 1)
    own = (lane >= p * ROWS) & (lane < (p + 1) * ROWS)
    mine_row = jnp.sum(jnp.where(own, row_lse, 0.0)) - 2.0 * matched
    part[...] = jnp.full((1, 128), mine_row, jnp.float32)
    own_c = (lane >= q * ROWS) & (lane < (q + 1) * ROWS)
    mine = mine_row + jnp.sum(jnp.where(own_c, col_lse, 0.0))
    parts_a[p] = jnp.full((1, 128), mine, jnp.float32)

    @pl.loop(1, G)
    def _(m):
        k = (p + m) % G
        copy(parts_a.at[p], parts_a.at[p], s_pa.at[k], r_pa.at[p], plane_dev(k)).start()

    col_loc = lax.broadcasted_iota(jnp.int32, (1, B), 1) - q * ROWS
    col_loc = jnp.where((col_loc >= 0) & (col_loc < ROWS), col_loc, -2)

    @pl.loop(0, T)
    def _(t):
        at = pl.ds(pl.multiple_of(t * TM, TM), TM)
        fr = rm_s[at, 0:1]
        fc = jnp.exp2(cm_s[t] - col_lse)
        row_loc = lax.broadcasted_iota(jnp.int32, (TM, 1), 0) + (t * TM - p * ROWS)
        row_loc = jnp.where((row_loc >= 0) & (row_loc < ROWS), row_loc, -1)
        ww = er[at, :] * fr + ec[at, :] * fc
        ww = jnp.where(row_loc == col_loc, ww - 2.0, ww)
        wb = ww.astype(jnp.bfloat16)
        w[at, :] = wb
        lp = jnp.dot(wb, rall[...], preferred_element_type=jnp.float32)
        for j in range(PER):
            k = t * PER + j
            ls[k] = lp[j * ROWS : (j + 1) * ROWS, :].astype(jnp.bfloat16)

            @pl.when(k != p)
            def _():
                copy(ls.at[k], lr.at[p], s_ls.at[k], r_ls.at[p], plane_dev(k)).start()

            @pl.when(k == p)
            def _():
                lgrad_ref[...] = lp[j * ROWS : (j + 1) * ROWS, :]

    @pl.loop(0, 3)
    def _(u):
        at = pl.ds(pl.multiple_of(u * 384, 384), 384)
        rp[at, :] = lax.dot_general(
            w[:, at], lall[...], (((0,), (0,)), ((), ())), preferred_element_type=jnp.float32
        )

    @pl.loop(0, G)
    def _(k):
        piece = rp[pl.ds(pl.multiple_of(k * ROWS, ROWS), ROWS), :]
        rs[k] = piece.astype(jnp.bfloat16)

        @pl.when(k != q)
        def _():
            copy(rs.at[k], rr.at[q], s_rs.at[k], r_rs.at[q], line_dev(k)).start()

        @pl.when(k == q)
        def _():
            rgrad_ref[...] = piece

    @pl.loop(1, G)
    def _(m):
        k = (p + m) % G
        copy(parts_a.at[p], parts_a.at[k], s_pa.at[k], r_pa.at[k], plane_dev(k)).wait()

    parts_b[q] = jnp.sum(parts_a[...], axis=0)

    @pl.loop(1, G)
    def _(m):
        k = (q + m) % G
        copy(parts_b.at[q], parts_b.at[q], s_pb.at[k], r_pb.at[q], line_dev(k)).start()

    @pl.loop(1, G)
    def _(m):
        k = (p + m) % G
        copy(ls.at[k], lr.at[k], s_ls.at[k], r_ls.at[k], plane_dev(k)).wait()
        lgrad_ref[...] += lr[k].astype(jnp.float32)

    @pl.loop(1, G)
    def _(m):
        k = (q + m) % G
        copy(rs.at[k], rr.at[k], s_rs.at[k], r_rs.at[k], line_dev(k)).wait()
        rgrad_ref[...] += rr[k].astype(jnp.float32)

    @pl.loop(1, G)
    def _(m):
        k = (q + m) % G
        copy(parts_b.at[q], parts_b.at[k], s_pb.at[k], r_pb.at[k], line_dev(k)).wait()

    loss_ref[...] = jnp.sum(parts_b[...], axis=0) * (LN2 / (2.0 * G * G * ROWS))


def shards(left, right):
    f32, bf16 = jnp.float32, jnp.bfloat16
    vmem = pl.BlockSpec(memory_space=pltpu.VMEM)
    dma = pltpu.SemaphoreType.DMA
    left_grad, right_grad, loss = pl.pallas_call(
        kernel,
        out_shape=(
            jax.ShapeDtypeStruct((ROWS, D), f32),
            jax.ShapeDtypeStruct((ROWS, D), f32),
            jax.ShapeDtypeStruct((1, 128), f32),
        ),
        in_specs=[vmem, vmem],
        out_specs=(vmem, vmem, vmem),
        scratch_shapes=[
            pltpu.VMEM((G, ROWS, D), bf16),
            pltpu.VMEM((G, ROWS, D), bf16),
            pltpu.VMEM((B, D), bf16),
            pltpu.VMEM((B, D), bf16),
            pltpu.VMEM((B, B), f32),
            pltpu.VMEM((B, B), f32),
            pltpu.VMEM((B, B), bf16),
            pltpu.VMEM((B, 128), f32),
            pltpu.VMEM((B, 128), f32),
            pltpu.VMEM((T, 1, B), f32),
            pltpu.VMEM((T, 1, B), f32),
            pltpu.VMEM((B, D), f32),
            pltpu.VMEM((G, 1, B), f32),
            pltpu.VMEM((G, 1, B), f32),
            pltpu.VMEM((G, ROWS, D), bf16),
            pltpu.VMEM((G, ROWS, D), bf16),
            pltpu.VMEM((G, ROWS, D), bf16),
            pltpu.VMEM((G, ROWS, D), bf16),
            pltpu.VMEM((1, 128), f32),
            pltpu.VMEM((G, 1, 128), f32),
            pltpu.VMEM((G, 1, 128), f32),
            dma((G,)), dma((G,)), dma((G,)), dma((G,)),
            dma((2 * G,)), dma((2 * G,)),
            dma((G,)), dma((G,)), dma((G,)), dma((G,)),
            dma((G,)), dma((G,)), dma((G,)), dma((G,)),
        ],
        compiler_params=pltpu.CompilerParams(
            collective_id=0, has_side_effects=True, vmem_limit_bytes=56 * 2**20
        ),
        cost_estimate=pl.CostEstimate(flops=6 * B * B * D, bytes_accessed=4 * ROWS * D * 4, transcendentals=2 * B * B),
        name="infonce",
    )(left, right)
    return left_grad, right_grad, loss[0, 0]


def solution(mesh):
    return jax.shard_map(
        shards,
        mesh=mesh,
        in_specs=(P("dp", None), P("dp", None)),
        out_specs=(P("dp", None), P("dp", None), P()),
        check_vma=False,
    )
```

```python
import math

import jax
import jax.numpy as jnp
from jax import lax
from jax.experimental import pallas as pl
from jax.experimental.pallas import tpu as pltpu
from jax.sharding import PartitionSpec as P

MESH = pl.DeviceIdType.MESH
NZ = 8
NA = 4
G = 16
ROWS = 72
D = 384
B = G * ROWS
TM = 4 * ROWS
CHUNKS = B // TM
TN = 384
LOG2E = math.log2(math.e)
LN2 = math.log(2.0)

A_OFFS = (2, 1, 3)
PLANE_OFFS = sorted(
    [(i, j) for i in range(NA) for j in range(NA) if (i, j) != (0, 0)],
    key=lambda o: -(min(o[0], NA - o[0]) + min(o[1], NA - o[1])),
)
LINE_OFFS = sorted(
    [(i, j) for i in range(NZ) for j in range(2) if (i, j) != (0, 0)],
    key=lambda o: -min(o[0], NZ - o[0]),
)


def kernel(
    left_ref, right_ref, lgrad_ref, rgrad_ref, loss_ref,
    lin, rin, lg, rg, lall, rall, er, ec, w, rm_s, rl_s, cm_s, cs_s, rp, ap,
    row_stat, col_stat, bs, br, sib_s, sib_r, zs, zr, zm, part_a, part_b,
    s_in, s_l, r_l, s_sib, r_sib, s_r, r_r, s_f, s_row, r_row, s_col, r_col,
    s_gb, r_gb, s_gs, r_gs, s_gz, r_gz, r_gm, s_pa, r_pa, s_pb, r_pb,
):
    me = lax.axis_index("dp")
    core = me % 2
    x = (me // 2) % NA
    y = (me // (2 * NA)) % NA
    z = me // (2 * G)
    a = y * (1 - core) + x * core
    b = x * (1 - core) + y * core
    step_a = 8 - 6 * core
    step_b = 2 + 6 * core
    p = a * NA + b
    q = z * 2 + core
    other = 1 - core
    sg = 1 - 2 * core
    scale = 2.0 / math.sqrt(D) * LOG2E

    def plane_dev(pa, pb):
        return (z * (2 * G) + pa * step_a + pb * step_b + core,)

    def line_dev(pz, pc):
        return (pz * (2 * G) + (y * NA + x) * 2 + pc,)

    def zz(d):
        return (z + d + NZ) % NZ

    sends = []

    def copy(src, dst, send, recv, dev):
        return pltpu.make_async_remote_copy(
            src_ref=src, dst_ref=dst, send_sem=send, recv_sem=recv, device_id=dev, device_id_type=MESH
        )

    def go(src, dst, send, recv, dev):
        c = copy(src, dst, send, recv, dev)
        c.start()
        sends.append(c)

    c_left = pltpu.make_async_copy(left_ref, lin, s_in.at[0])
    c_right = pltpu.make_async_copy(right_ref, rin, s_in.at[1])
    c_left.start()
    c_right.start()
    barrier = pltpu.get_barrier_semaphore()
    for i in range(G - 1):
        da, db = PLANE_OFFS[i]
        dev = plane_dev((a + da) % NA, (b + db) % NA)
        pl.semaphore_signal(barrier, inc=1, device_id=dev, device_id_type=MESH)
        dz, dc = LINE_OFFS[i]
        dev = line_dev((z + dz) % NZ, (core + dc) % 2)
        pl.semaphore_signal(barrier, inc=1, device_id=dev, device_id_type=MESH)
    c_left.wait()
    c_right.wait()
    lbf = lin[...].astype(jnp.bfloat16)
    rbf = rin[...].astype(jnp.bfloat16)
    lg[q] = lbf
    rg[p] = rbf
    matched = jnp.sum(lbf.astype(jnp.float32) * rbf.astype(jnp.float32)) * scale
    pl.semaphore_wait(barrier, 2 * (G - 1))

    def line_slot(k, c):
        return lg.at[k * 2 + c]

    def line_wait(d):
        k = zz(d)
        copy(lg.at[q], line_slot(k, core), s_l.at[0], r_l.at[k], line_dev(k, core)).wait_recv()
        return k

    def to_sibling(k):
        piece = line_slot(k, core)
        go(piece, piece, s_sib.at[k], r_sib.at[k], line_dev(z, other))

    def relay(k, i, d):
        piece = line_slot(k, core)
        go(piece, piece, s_l.at[i], r_l.at[k], line_dev(zz(d), core))

    def plane_wait(ka, kb):
        k = ka * NA + kb
        copy(rg.at[p], rg.at[k], s_r.at[0], r_r.at[k], plane_dev(ka, kb)).wait_recv()
        return k

    for i, d in enumerate((2, -2, 1, -1)):
        go(lg.at[q], lg.at[q], s_l.at[i], r_l.at[z], line_dev(zz(d), core))
    for i, d in enumerate(A_OFFS):
        go(rg.at[p], rg.at[p], s_r.at[i], r_r.at[p], plane_dev(a, (b + d) % NA))
    for i, d in enumerate(A_OFFS):
        go(rg.at[p], rg.at[p], s_r.at[3 + i], r_r.at[p], plane_dev((a + d) % NA, b))
    to_sibling(z)
    for n, db in enumerate((1, 3, 2)):
        k = plane_wait(a, (b + db) % NA)
        for i, d in enumerate(A_OFFS):
            go(rg.at[k], rg.at[k], s_f.at[n * 3 + i], r_r.at[k], plane_dev((a + d) % NA, b))
    k = line_wait(-2 * sg)
    relay(k, 4, 2 * sg)
    relay(k, 5, sg)
    k2 = line_wait(2 * sg)
    relay(k2, 6, -sg)
    to_sibling(k)
    to_sibling(k2)
    for d in (1, -1, 3 * sg, -3 * sg, 4):
        to_sibling(line_wait(d))
    for da in (1, 3, 2):
        for db in (0, 1, 3, 2):
            plane_wait((a + da) % NA, (b + db) % NA)

    def join(src, k, dst, at):
        two = [src[k].astype(jnp.float32), src[k + 1].astype(jnp.float32)]
        dst[pl.ds(pl.multiple_of(at, 2 * ROWS), 2 * ROWS), :] = jnp.concatenate(two, axis=0).astype(jnp.bfloat16)

    @pl.loop(0, G // 2)
    def _(j):
        join(rg, 2 * j, rall, j * 2 * ROWS)

    zp = z // 2
    near = 1 - 2 * (z % 2)

    def scores(t):
        for j in range(2):
            k = 2 * t + j
            copy(lg.at[q], line_slot(k, other), s_sib.at[0], r_sib.at[k], line_dev(z, other)).wait_recv()
            join(lg, 2 * k, lall, k * 2 * ROWS)
        at = pl.ds(pl.multiple_of(t * TM, TM), TM)
        s = lax.dot_general(
            lall[at, :], rall[...], (((1,), (1,)), ((), ())), preferred_element_type=jnp.float32
        ) * scale
        rm = jnp.max(s, axis=1, keepdims=True)
        e = jnp.exp2(s - rm)
        er[at, :] = e
        rm_s[at, :] = jnp.broadcast_to(rm, (TM, 128))
        rl_s[at, :] = jnp.broadcast_to(rm + jnp.log2(jnp.sum(e, axis=1, keepdims=True)), (TM, 128))
        cm = jnp.max(s, axis=0, keepdims=True)
        e = jnp.exp2(s - cm)
        ec[at, :] = e
        cm_s[t] = cm
        cs_s[t] = jnp.sum(e, axis=0, keepdims=True)

    @pl.loop(0, CHUNKS)
    def _(o):
        shift = (o % 2) * (1 - o // 2) * near - (o // 2) * (1 - o % 2) * near + (o // 2) * (o % 2) * 2
        scores((zp + shift + CHUNKS) % CHUNKS)

    cm = jnp.max(cm_s[...], axis=0)
    cs = jnp.sum(cs_s[...] * jnp.exp2(cm_s[...] - cm[None]), axis=0)
    col_stat[p, :, 0:B] = cm + jnp.log2(cs)
    col_stat[p, :, B : B + 128] = jnp.full((1, 128), matched, jnp.float32)
    row_stat[q] = jnp.transpose(rl_s[...])[0:1, :]

    for i in range(G - 1):
        dz, dc = LINE_OFFS[i]
        dev = line_dev((z + dz) % NZ, (core + dc) % 2)
        go(row_stat.at[q], row_stat.at[q], s_row.at[i], r_row.at[q], dev)
        da, db = PLANE_OFFS[i]
        dev = plane_dev((a + da) % NA, (b + db) % NA)
        go(col_stat.at[p], col_stat.at[p], s_col.at[i], r_col.at[p], dev)
    for i in range(G - 1):
        dz, dc = LINE_OFFS[-1 - i]
        kz, kc = (z + dz) % NZ, (core + dc) % 2
        k = kz * 2 + kc
        copy(row_stat.at[q], row_stat.at[k], s_row.at[i], r_row.at[k], line_dev(kz, kc)).wait_recv()
        da, db = PLANE_OFFS[-1 - i]
        ka, kb = (a + da) % NA, (b + db) % NA
        k = ka * NA + kb
        copy(col_stat.at[p], col_stat.at[k], s_col.at[i], r_col.at[k], plane_dev(ka, kb)).wait_recv()

    def combine(v):
        top = jnp.max(v, axis=0)
        return top + jnp.log2(jnp.sum(jnp.exp2(v - top[None]), axis=0))

    row_lse = combine(row_stat[...])
    col_lse = combine(col_stat[:, :, 0:B])
    rm_s[...] = jnp.exp2(rm_s[...] - jnp.transpose(jnp.broadcast_to(row_lse, (128, B))))

    pairs = jnp.sum(col_stat[:, :, B : B + 128], axis=0)
    part_a[q] = jnp.sum(col_lse) - 2.0 * pairs
    part_b[p] = jnp.full((1, 128), jnp.sum(row_lse), jnp.float32)

    col_loc = lax.broadcasted_iota(jnp.int32, (1, B), 1) - p * ROWS
    col_loc = jnp.where((col_loc >= 0) & (col_loc < ROWS), col_loc, -2)

    @pl.loop(0, CHUNKS)
    def _(t):
        at = pl.ds(pl.multiple_of(t * TM, TM), TM)
        fc = jnp.exp2(cm_s[t] - col_lse)
        row_loc = lax.broadcasted_iota(jnp.int32, (TM, 1), 0) + (t * TM - q * ROWS)
        row_loc = jnp.where((row_loc >= 0) & (row_loc < ROWS), row_loc, -1)
        ww = er[at, :] * rm_s[at, 0:1] + ec[at, :] * fc
        w[at, :] = jnp.where(row_loc == col_loc, ww - 2.0, ww).astype(jnp.bfloat16)

    first = 0
    for u in range(B // TN):
        rp[u * TN : (u + 1) * TN, :] = lax.dot_general(
            w[:, u * TN : (u + 1) * TN], lall[...], (((0,), (0,)), ((), ())), preferred_element_type=jnp.float32
        )
        last = (u + 1) * TN // ROWS

        @pl.loop(first, last)
        def _(k):
            piece = rp[pl.ds(pl.multiple_of(k * ROWS, ROWS), ROWS), :]
            bs[k] = piece.astype(jnp.bfloat16)

            @pl.when(k != p)
            def _():
                copy(bs.at[k], br.at[p], s_gb.at[k], r_gb.at[p], plane_dev(k // NA, k % NA)).start()

            @pl.when(k == p)
            def _():
                rgrad_ref[...] = piece

        first = last

    @pl.loop(0, CHUNKS)
    def _(o):
        back = 3 - o
        shift = (back % 2) * (1 - back // 2) * near - (back // 2) * (1 - back % 2) * near + (back // 2) * (back % 2) * 2
        t = (zp + shift + CHUNKS) % CHUNKS
        at = pl.ds(pl.multiple_of(t * TM, TM), TM)
        part = jnp.dot(w[at, :], rall[...], preferred_element_type=jnp.float32)
        for j in range(2):
            k = 2 * t + j
            lo = part[2 * j * ROWS : (2 * j + 1) * ROWS, :]
            hi = part[(2 * j + 1) * ROWS : (2 * j + 2) * ROWS, :]
            mine = jnp.where(core == 0, lo, hi)
            yours = jnp.where(core == 0, hi, lo)
            ap[k] = mine
            sib_s[k] = yours.astype(jnp.bfloat16)
            copy(sib_s.at[k], sib_r.at[k], s_gs.at[k], r_gs.at[k], line_dev(z, other)).start()

    def chip_sum(k):
        copy(sib_s.at[k], sib_r.at[k], s_gs.at[k], r_gs.at[k], line_dev(z, other)).wait_recv()
        return ap[k] + sib_r[k].astype(jnp.float32)

    def mid(i, owner, d):
        zs[i] = chip_sum(zz(owner)).astype(jnp.bfloat16)
        go(zs.at[i], zm.at[i], s_gz.at[i], r_gm.at[i], line_dev(zz(d), core))

    def mid_wait(i):
        copy(zs.at[i], zm.at[i], s_gz.at[i], r_gm.at[i], line_dev(z, other)).wait_recv()
        return zm[i].astype(jnp.float32)

    def end(i, d, value):
        zs[i] = value.astype(jnp.bfloat16)
        go(zs.at[i], zr.at[i - 3], s_gz.at[i], r_gz.at[i - 3], line_dev(zz(d), core))

    mid(0, 4, -2 * sg)
    mid(1, -3 * sg, -sg)
    mid(2, 3 * sg, sg)
    end(3, 1, chip_sum(zz(1)))
    end(4, -1, chip_sum(zz(-1)))
    plus = chip_sum(zz(2 * sg))
    minus = chip_sum(zz(-2 * sg))
    lgrad_ref[...] = chip_sum(z)
    end(5, 2 * sg, plus + mid_wait(2))
    end(6, -2 * sg, minus + mid_wait(0) + mid_wait(1))

    for i in range(G - 1):
        da, db = PLANE_OFFS[i]
        dev = plane_dev((a + da) % NA, (b + db) % NA)
        go(part_b.at[p], part_b.at[p], s_pb.at[i], r_pb.at[p], dev)
        dz, dc = LINE_OFFS[i]
        dev = line_dev((z + dz) % NZ, (core + dc) % 2)
        go(part_a.at[q], part_a.at[q], s_pa.at[i], r_pa.at[q], dev)
    for da, db in reversed(PLANE_OFFS):
        ka, kb = (a + da) % NA, (b + db) % NA
        k = ka * NA + kb
        copy(bs.at[k], br.at[k], s_gb.at[k], r_gb.at[k], plane_dev(ka, kb)).wait()
        rgrad_ref[...] += br[k].astype(jnp.float32)
    for i in range(G - 1):
        da, db = PLANE_OFFS[i]
        ka, kb = (a + da) % NA, (b + db) % NA
        k = ka * NA + kb
        copy(part_b.at[p], part_b.at[k], s_pb.at[i], r_pb.at[k], plane_dev(ka, kb)).wait_recv()
        dz, dc = LINE_OFFS[i]
        kz, kc = (z + dz) % NZ, (core + dc) % 2
        k = kz * 2 + kc
        copy(part_a.at[q], part_a.at[k], s_pa.at[i], r_pa.at[k], line_dev(kz, kc)).wait_recv()
    loss_ref[...] = (jnp.sum(part_a[...], axis=0) + jnp.sum(part_b[...], axis=0)) * (LN2 / (2.0 * NZ * 2 * B))
    for i in range(4):
        copy(zs.at[3 + i], zr.at[i], s_gz.at[i], r_gz.at[i], line_dev(z, other)).wait_recv()
        lgrad_ref[...] += zr[i].astype(jnp.float32)
    for k in range(NZ):
        copy(sib_s.at[k], sib_r.at[k], s_gs.at[k], r_gs.at[k], line_dev(z, other)).wait_send()
    for c in sends:
        c.wait_send()


def shards(left, right):
    f32, bf16 = jnp.float32, jnp.bfloat16
    anywhere = pl.BlockSpec(memory_space=pl.ANY)
    vmem = pl.BlockSpec(memory_space=pltpu.VMEM)
    dma = pltpu.SemaphoreType.DMA
    left_grad, right_grad, loss = pl.pallas_call(
        kernel,
        out_shape=(pltpu.VMEM((ROWS, D), f32), pltpu.VMEM((ROWS, D), f32), pltpu.VMEM((1, 128), f32)),
        in_specs=[anywhere, anywhere],
        out_specs=(vmem, vmem, vmem),
        scratch_shapes=[
            pltpu.VMEM((ROWS, D), f32),
            pltpu.VMEM((ROWS, D), f32),
            pltpu.VMEM((G, ROWS, D), bf16),
            pltpu.VMEM((G, ROWS, D), bf16),
            pltpu.VMEM((B, D), bf16),
            pltpu.VMEM((B, D), bf16),
            pltpu.VMEM((B, B), f32),
            pltpu.VMEM((B, B), f32),
            pltpu.VMEM((B, B), bf16),
            pltpu.VMEM((B, 128), f32),
            pltpu.VMEM((B, 128), f32),
            pltpu.VMEM((CHUNKS, 1, B), f32),
            pltpu.VMEM((CHUNKS, 1, B), f32),
            pltpu.VMEM((B, D), f32),
            pltpu.VMEM((NZ, ROWS, D), f32),
            pltpu.VMEM((G, 1, B), f32),
            pltpu.VMEM((G, 1, B + 128), f32),
            pltpu.VMEM((G, ROWS, D), bf16),
            pltpu.VMEM((G, ROWS, D), bf16),
            pltpu.VMEM((NZ, ROWS, D), bf16),
            pltpu.VMEM((NZ, ROWS, D), bf16),
            pltpu.VMEM((7, ROWS, D), bf16),
            pltpu.VMEM((4, ROWS, D), bf16),
            pltpu.VMEM((3, ROWS, D), bf16),
            pltpu.VMEM((G, 1, 128), f32),
            pltpu.VMEM((G, 1, 128), f32),
            dma((2,)),
            dma((NZ,)), dma((NZ,)),
            dma((NZ,)), dma((NZ,)),
            dma((6,)), dma((G,)),
            dma((9,)),
            dma((G,)), dma((G,)),
            dma((G,)), dma((G,)),
            dma((G,)), dma((G,)),
            dma((NZ,)), dma((NZ,)),
            dma((7,)), dma((4,)), dma((3,)),
            dma((G,)), dma((G,)),
            dma((G,)), dma((G,)),
        ],
        compiler_params=pltpu.CompilerParams(
            collective_id=0, has_side_effects=True, vmem_limit_bytes=56 * 2**20
        ),
        cost_estimate=pl.CostEstimate(flops=6 * B * B * D, bytes_accessed=16 * ROWS * D, transcendentals=2 * B * B),
        name="infonce",
    )(left, right)
    return left_grad, right_grad, loss[0, 0]


def solution(mesh):
    return jax.shard_map(
        shards,
        mesh=mesh,
        in_specs=(P("dp", None), P("dp", None)),
        out_specs=(P("dp", None), P("dp", None), P()),
        check_vma=False,
    )
```

```python
import math

import jax
import jax.numpy as jnp
from jax import lax
from jax.experimental import pallas as pl
from jax.experimental.pallas import tpu as pltpu
from jax.sharding import PartitionSpec as P

MESH = pl.DeviceIdType.MESH
NZ = 8
NA = 4
G = 16
ROWS = 72
D = 384
B = G * ROWS
TM = 4 * ROWS
CHUNKS = B // TM
TN = 384
LOG2E = math.log2(math.e)
LN2 = math.log(2.0)

A_OFFS = (2, 1, 3)
PLANE_OFFS = sorted(
    [(i, j) for i in range(NA) for j in range(NA) if (i, j) != (0, 0)],
    key=lambda o: -(min(o[0], NA - o[0]) + min(o[1], NA - o[1])),
)
LINE_OFFS = sorted(
    [(i, j) for i in range(NZ) for j in range(2) if (i, j) != (0, 0)],
    key=lambda o: -min(o[0], NZ - o[0]),
)


def kernel(
    left_ref, right_ref, lgrad_ref, rgrad_ref, loss_ref,
    lin, rin, lg, rg, lall, rall, er, ec, w, rm_s, rl_s, cm_s, cs_s, rp, ap,
    row_stat, col_stat, bs, br, ls, lr, sib_s, sib_r, zs, zr, zm, part_a, part_b,
    s_in, s_l, r_l, s_sib, r_sib, s_r, r_r, s_f, s_row, r_row, s_col, r_col,
    s_gb, r_gb, s_gl, r_gl, s_gs, r_gs, s_gz, r_gz, r_gm, s_pa, r_pa, s_pb, r_pb,
):
    me = lax.axis_index("dp")
    core = me % 2
    x = (me // 2) % NA
    y = (me // (2 * NA)) % NA
    z = me // (2 * G)
    a = y * (1 - core) + x * core
    b = x * (1 - core) + y * core
    step_a = 8 - 6 * core
    step_b = 2 + 6 * core
    p = a * NA + b
    q = z * 2 + core
    other = 1 - core
    sg = 1 - 2 * core
    scale = 2.0 / math.sqrt(D) * LOG2E

    def plane_dev(pa, pb):
        return (z * (2 * G) + pa * step_a + pb * step_b + core,)

    def line_dev(pz, pc):
        return (pz * (2 * G) + (y * NA + x) * 2 + pc,)

    def zz(d):
        return (z + d + NZ) % NZ

    sends = []

    def copy(src, dst, send, recv, dev):
        return pltpu.make_async_remote_copy(
            src_ref=src, dst_ref=dst, send_sem=send, recv_sem=recv, device_id=dev, device_id_type=MESH
        )

    def go(src, dst, send, recv, dev):
        c = copy(src, dst, send, recv, dev)
        c.start()
        sends.append(c)

    c_left = pltpu.make_async_copy(left_ref, lin, s_in.at[0])
    c_right = pltpu.make_async_copy(right_ref, rin, s_in.at[1])
    c_left.start()
    c_right.start()
    barrier = pltpu.get_barrier_semaphore()
    firsts = [plane_dev((a + d) % NA, b) for d in A_OFFS] + [plane_dev(a, (b + d) % NA) for d in A_OFFS]
    firsts += [line_dev(zz(d), core) for d in (2, -2, 1, -1)] + [line_dev(z, other)]
    for dev in firsts:
        pl.semaphore_signal(barrier, inc=1, device_id=dev, device_id_type=MESH)
    c_left.wait()
    c_right.wait()
    lbf = lin[...].astype(jnp.bfloat16)
    rbf = rin[...].astype(jnp.bfloat16)
    lg[q] = lbf
    rg[p] = rbf
    matched = jnp.sum(lbf.astype(jnp.float32) * rbf.astype(jnp.float32)) * scale
    pl.semaphore_wait(barrier, len(firsts))

    def line_slot(k, c):
        return lg.at[k * 2 + c]

    def line_wait(d):
        k = zz(d)
        copy(lg.at[q], line_slot(k, core), s_l.at[0], r_l.at[k], line_dev(k, core)).wait_recv()
        return k

    def to_sibling(k):
        piece = line_slot(k, core)
        go(piece, piece, s_sib.at[k], r_sib.at[k], line_dev(z, other))

    def relay(k, i, d):
        piece = line_slot(k, core)
        go(piece, piece, s_l.at[i], r_l.at[k], line_dev(zz(d), core))

    def plane_wait(ka, kb):
        k = ka * NA + kb
        copy(rg.at[p], rg.at[k], s_r.at[0], r_r.at[k], plane_dev(ka, kb)).wait_recv()
        return k

    for i, d in enumerate((2, -2, 1, -1)):
        go(lg.at[q], lg.at[q], s_l.at[i], r_l.at[z], line_dev(zz(d), core))
    for i, d in enumerate(A_OFFS):
        go(rg.at[p], rg.at[p], s_r.at[i], r_r.at[p], plane_dev(a, (b + d) % NA))
    for i, d in enumerate(A_OFFS):
        go(rg.at[p], rg.at[p], s_r.at[3 + i], r_r.at[p], plane_dev((a + d) % NA, b))
    to_sibling(z)
    for n, db in enumerate((1, 3, 2)):
        k = plane_wait(a, (b + db) % NA)
        for i, d in enumerate(A_OFFS):
            go(rg.at[k], rg.at[k], s_f.at[n * 3 + i], r_r.at[k], plane_dev((a + d) % NA, b))
    k = line_wait(-2 * sg)
    relay(k, 4, 2 * sg)
    relay(k, 5, sg)
    k2 = line_wait(2 * sg)
    relay(k2, 6, -sg)
    to_sibling(k)
    to_sibling(k2)
    for d in (1, -1, 3 * sg, -3 * sg, 4):
        to_sibling(line_wait(d))
    for da in (1, 3, 2):
        for db in (0, 1, 3, 2):
            plane_wait((a + da) % NA, (b + db) % NA)

    def join(src, k, dst, at):
        two = [src[k].astype(jnp.float32), src[k + 1].astype(jnp.float32)]
        dst[pl.ds(pl.multiple_of(at, 2 * ROWS), 2 * ROWS), :] = jnp.concatenate(two, axis=0).astype(jnp.bfloat16)

    @pl.loop(0, G // 2)
    def _(j):
        join(rg, 2 * j, rall, j * 2 * ROWS)

    zp = z // 2
    near = 1 - 2 * (z % 2)

    def scores(t):
        for j in range(2):
            k = 2 * t + j
            copy(lg.at[q], line_slot(k, other), s_sib.at[0], r_sib.at[k], line_dev(z, other)).wait_recv()
            join(lg, 2 * k, lall, k * 2 * ROWS)
        at = pl.ds(pl.multiple_of(t * TM, TM), TM)
        s = lax.dot_general(
            lall[at, :], rall[...], (((1,), (1,)), ((), ())), preferred_element_type=jnp.float32
        ) * scale
        rm = jnp.max(s, axis=1, keepdims=True)
        e = jnp.exp2(s - rm)
        er[at, :] = e
        rm_s[at, :] = jnp.broadcast_to(rm, (TM, 128))
        rl_s[at, :] = jnp.broadcast_to(rm + jnp.log2(jnp.sum(e, axis=1, keepdims=True)), (TM, 128))
        cm = jnp.max(s, axis=0, keepdims=True)
        e = jnp.exp2(s - cm)
        ec[at, :] = e
        cm_s[t] = cm
        cs_s[t] = jnp.sum(e, axis=0, keepdims=True)

    @pl.loop(0, CHUNKS)
    def _(o):
        shift = (o % 2) * (1 - o // 2) * near - (o // 2) * (1 - o % 2) * near + (o // 2) * (o % 2) * 2
        scores((zp + shift + CHUNKS) % CHUNKS)

    cm = jnp.max(cm_s[...], axis=0)
    cs = jnp.sum(cs_s[...] * jnp.exp2(cm_s[...] - cm[None]), axis=0)
    col_stat[p, :, 0:B] = cm + jnp.log2(cs)
    col_stat[p, :, B : B + 128] = jnp.full((1, 128), matched, jnp.float32)
    row_stat[q] = jnp.transpose(rl_s[...])[0:1, :]

    for i in range(G - 1):
        dz, dc = LINE_OFFS[i]
        dev = line_dev((z + dz) % NZ, (core + dc) % 2)
        go(row_stat.at[q], row_stat.at[q], s_row.at[i], r_row.at[q], dev)
        da, db = PLANE_OFFS[i]
        dev = plane_dev((a + da) % NA, (b + db) % NA)
        go(col_stat.at[p], col_stat.at[p], s_col.at[i], r_col.at[p], dev)
    for i in range(G - 1):
        dz, dc = LINE_OFFS[-1 - i]
        kz, kc = (z + dz) % NZ, (core + dc) % 2
        k = kz * 2 + kc
        copy(row_stat.at[q], row_stat.at[k], s_row.at[i], r_row.at[k], line_dev(kz, kc)).wait_recv()
        da, db = PLANE_OFFS[-1 - i]
        ka, kb = (a + da) % NA, (b + db) % NA
        k = ka * NA + kb
        copy(col_stat.at[p], col_stat.at[k], s_col.at[i], r_col.at[k], plane_dev(ka, kb)).wait_recv()

    def combine(v):
        top = jnp.max(v, axis=0)
        return top + jnp.log2(jnp.sum(jnp.exp2(v - top[None]), axis=0))

    row_lse = combine(row_stat[...])
    col_lse = combine(col_stat[:, :, 0:B])
    rm_s[...] = jnp.exp2(rm_s[...] - jnp.transpose(jnp.broadcast_to(row_lse, (128, B))))

    pairs = jnp.sum(col_stat[:, :, B : B + 128], axis=0)
    part_a[q] = jnp.sum(col_lse) - 2.0 * pairs
    part_b[p] = jnp.full((1, 128), jnp.sum(row_lse), jnp.float32)

    col_loc = lax.broadcasted_iota(jnp.int32, (1, B), 1) - p * ROWS
    col_loc = jnp.where((col_loc >= 0) & (col_loc < ROWS), col_loc, -2)

    for i, d in enumerate(A_OFFS):
        go(part_b.at[p], part_b.at[p], s_pb.at[i], r_pb.at[p], plane_dev(a, (b + d) % NA))
    go(part_a.at[q], part_a.at[q], s_pa.at[0], r_pa.at[q], line_dev(z, other))
    @pl.loop(0, CHUNKS)
    def _(t):
        at = pl.ds(pl.multiple_of(t * TM, TM), TM)
        fc = jnp.exp2(cm_s[t] - col_lse)
        row_loc = lax.broadcasted_iota(jnp.int32, (TM, 1), 0) + (t * TM - q * ROWS)
        row_loc = jnp.where((row_loc >= 0) & (row_loc < ROWS), row_loc, -1)
        ww = er[at, :] * rm_s[at, 0:1] + ec[at, :] * fc
        w[at, :] = jnp.where(row_loc == col_loc, ww - 2.0, ww).astype(jnp.bfloat16)

    def right_step(u):
        rp[u * TN : (u + 1) * TN, :] = lax.dot_general(
            w[:, u * TN : (u + 1) * TN], lall[...], (((0,), (0,)), ((), ())), preferred_element_type=jnp.float32
        )
        for k in range(u * TN // ROWS, (u + 1) * TN // ROWS):
            ka, kb = k // NA, k % NA

            @pl.when(ka != a)
            def _():
                bs[k] = rp[k * ROWS : (k + 1) * ROWS, :].astype(jnp.bfloat16)
                mine = a * NA + kb
                copy(bs.at[k], br.at[mine], s_gb.at[k], r_gb.at[mine], plane_dev(ka, b)).start()

    def left_step(shift):
        t = (zp + shift + CHUNKS) % CHUNKS
        at = pl.ds(pl.multiple_of(t * TM, TM), TM)
        part = jnp.dot(w[at, :], rall[...], preferred_element_type=jnp.float32)
        for j in range(2):
            k = 2 * t + j
            lo = part[2 * j * ROWS : (2 * j + 1) * ROWS, :]
            hi = part[(2 * j + 1) * ROWS : (2 * j + 2) * ROWS, :]
            ap[k] = jnp.where(core == 0, lo, hi)
            sib_s[k] = jnp.where(core == 0, hi, lo).astype(jnp.bfloat16)
            copy(sib_s.at[k], sib_r.at[k], s_gs.at[k], r_gs.at[k], line_dev(z, other)).start()

    def chip_sum(k):
        copy(sib_s.at[k], sib_r.at[k], s_gs.at[k], r_gs.at[k], line_dev(z, other)).wait_recv()
        return ap[k] + sib_r[k].astype(jnp.float32)

    def mid(i, owner, d):
        zs[i] = chip_sum(zz(owner)).astype(jnp.bfloat16)
        go(zs.at[i], zm.at[i], s_gz.at[i], r_gm.at[i], line_dev(zz(d), core))

    def mid_wait(i):
        copy(zs.at[i], zm.at[i], s_gz.at[i], r_gm.at[i], line_dev(z, other)).wait_recv()
        return zm[i].astype(jnp.float32)

    def end(i, d, value):
        zs[i] = value.astype(jnp.bfloat16)
        go(zs.at[i], zr.at[i - 3], s_gz.at[i], r_gz.at[i - 3], line_dev(zz(d), core))

    right_step(0)
    left_step(2)
    right_step(1)
    left_step(near)
    for d in A_OFFS:
        k = a * NA + (b + d) % NA
        copy(part_b.at[p], part_b.at[k], s_pb.at[0], r_pb.at[k], plane_dev(0, 0)).wait_recv()
    own = pl.ds(a * NA, NA)
    for i, d in enumerate(A_OFFS):
        dev = plane_dev((a + d) % NA, b)
        go(part_b.at[own], part_b.at[own], s_pb.at[3 + i], r_pa.at[G + a], dev)
    k = z * 2 + other
    copy(part_a.at[q], part_a.at[k], s_pa.at[0], r_pa.at[k], line_dev(z, other)).wait_recv()
    own = pl.ds(z * 2, 2)
    for i, d in enumerate((4, 3, -3, 2, -2, 1, -1)):
        go(part_a.at[own], part_a.at[own], s_pa.at[1 + i], r_pa.at[2 * G + z], line_dev(zz(d), core))
    right_step(2)
    mid(0, 4, -2 * sg)
    mid(1, -3 * sg, -sg)
    mid(2, 3 * sg, sg)
    left_step(-near)
    left_step(0)
    end(3, 1, chip_sum(zz(1)))
    end(4, -1, chip_sum(zz(-1)))
    plus = chip_sum(zz(2 * sg))
    minus = chip_sum(zz(-2 * sg))
    lgrad_ref[...] = chip_sum(z)
    end(5, 2 * sg, plus + mid_wait(2))
    end(6, -2 * sg, minus + mid_wait(0) + mid_wait(1))
    def right_sum(kb):
        k = a * NA + kb
        total = rp[pl.ds(pl.multiple_of(k * ROWS, ROWS), ROWS), :]
        for d in A_OFFS:
            k = (a + d) % NA * NA + kb
            copy(bs.at[k], br.at[k], s_gb.at[k], r_gb.at[k], plane_dev(0, 0)).wait()
            total += br[k].astype(jnp.float32)
        return total

    for i, d in enumerate(A_OFFS):
        kb = (b + d) % NA
        ls[i] = right_sum(kb).astype(jnp.bfloat16)
        go(ls.at[i], lr.at[b], s_gl.at[i], r_gl.at[b], plane_dev(a, kb))
    rgrad_ref[...] = right_sum(b)
    for i, d in enumerate(A_OFFS):
        copy(ls.at[i], lr.at[(b + d) % NA], s_gl.at[i], r_gl.at[(b + d) % NA], plane_dev(0, 0)).wait_recv()
        rgrad_ref[...] += lr[(b + d) % NA].astype(jnp.float32)
    for i in range(4):
        copy(zs.at[3 + i], zr.at[i], s_gz.at[i], r_gz.at[i], line_dev(z, other)).wait_recv()
        lgrad_ref[...] += zr[i].astype(jnp.float32)
    for d in A_OFFS:
        k = (a + d) % NA
        there = part_b.at[pl.ds(k * NA, NA)]
        copy(there, there, s_pb.at[0], r_pa.at[G + k], plane_dev(0, 0)).wait_recv()
    for d in (4, 3, -3, 2, -2, 1, -1):
        there = part_a.at[pl.ds(zz(d) * 2, 2)]
        copy(there, there, s_pa.at[0], r_pa.at[2 * G + zz(d)], line_dev(0, 0)).wait_recv()
    loss_ref[...] = (jnp.sum(part_a[...], axis=0) + jnp.sum(part_b[...], axis=0)) * (LN2 / (2.0 * NZ * 2 * B))
    for k in range(NZ):
        copy(sib_s.at[k], sib_r.at[k], s_gs.at[k], r_gs.at[k], line_dev(z, other)).wait_send()
    for c in sends:
        c.wait_send()


def shards(left, right):
    f32, bf16 = jnp.float32, jnp.bfloat16
    anywhere = pl.BlockSpec(memory_space=pl.ANY)
    vmem = pl.BlockSpec(memory_space=pltpu.VMEM)
    dma = pltpu.SemaphoreType.DMA
    left_grad, right_grad, loss = pl.pallas_call(
        kernel,
        out_shape=(pltpu.VMEM((ROWS, D), f32), pltpu.VMEM((ROWS, D), f32), pltpu.VMEM((1, 128), f32)),
        in_specs=[anywhere, anywhere],
        out_specs=(vmem, vmem, vmem),
        scratch_shapes=[
            pltpu.VMEM((ROWS, D), f32),
            pltpu.VMEM((ROWS, D), f32),
            pltpu.VMEM((G, ROWS, D), bf16),
            pltpu.VMEM((G, ROWS, D), bf16),
            pltpu.VMEM((B, D), bf16),
            pltpu.VMEM((B, D), bf16),
            pltpu.VMEM((B, B), f32),
            pltpu.VMEM((B, B), f32),
            pltpu.VMEM((B, B), bf16),
            pltpu.VMEM((B, 128), f32),
            pltpu.VMEM((B, 128), f32),
            pltpu.VMEM((CHUNKS, 1, B), f32),
            pltpu.VMEM((CHUNKS, 1, B), f32),
            pltpu.VMEM((B, D), f32),
            pltpu.VMEM((NZ, ROWS, D), f32),
            pltpu.VMEM((G, 1, B), f32),
            pltpu.VMEM((G, 1, B + 128), f32),
            pltpu.VMEM((G, ROWS, D), bf16),
            pltpu.VMEM((G, ROWS, D), bf16),
            pltpu.VMEM((3, ROWS, D), bf16),
            pltpu.VMEM((NA, ROWS, D), bf16),
            pltpu.VMEM((NZ, ROWS, D), bf16),
            pltpu.VMEM((NZ, ROWS, D), bf16),
            pltpu.VMEM((7, ROWS, D), bf16),
            pltpu.VMEM((4, ROWS, D), bf16),
            pltpu.VMEM((3, ROWS, D), bf16),
            pltpu.VMEM((G, 1, 128), f32),
            pltpu.VMEM((G, 1, 128), f32),
            dma((2,)),
            dma((NZ,)), dma((NZ,)),
            dma((NZ,)), dma((NZ,)),
            dma((6,)), dma((G,)),
            dma((9,)),
            dma((G,)), dma((G,)),
            dma((G,)), dma((G,)),
            dma((G,)), dma((G,)),
            dma((3,)), dma((NA,)),
            dma((NZ,)), dma((NZ,)),
            dma((7,)), dma((4,)), dma((3,)),
            dma((G,)), dma((3 * G,)),
            dma((G,)), dma((G,)),
        ],
        compiler_params=pltpu.CompilerParams(
            collective_id=0, has_side_effects=True, vmem_limit_bytes=56 * 2**20
        ),
        cost_estimate=pl.CostEstimate(flops=6 * B * B * D, bytes_accessed=16 * ROWS * D, transcendentals=2 * B * B),
        name="infonce",
    )(left, right)
    return left_grad, right_grad, loss[0, 0]


def solution(mesh):
    return jax.shard_map(
        shards,
        mesh=mesh,
        in_specs=(P("dp", None), P("dp", None)),
        out_specs=(P("dp", None), P("dp", None), P()),
        check_vma=False,
    )
```

```python
import math

import jax
import jax.numpy as jnp
from jax import lax
from jax.experimental import pallas as pl
from jax.experimental.pallas import tpu as pltpu
from jax.sharding import PartitionSpec as P

MESH = pl.DeviceIdType.MESH
NZ = 8
NA = 4
G = 16
ROWS = 72
D = 384
B = G * ROWS
TM = 4 * ROWS
CHUNKS = B // TM
TN = 384
LOG2E = math.log2(math.e)
LN2 = math.log(2.0)

A_OFFS = (2, 1, 3)
BUNDLES = (2, 1, 3, 0)
PLACE = (3, 1, 0, 2)
NEAR_FIRST = (1, 2, 0, 3)
PLANE_OFFS = sorted(
    [(i, j) for i in range(NA) for j in range(NA) if (i, j) != (0, 0)],
    key=lambda o: -(min(o[0], NA - o[0]) + min(o[1], NA - o[1])),
)
LINE_OFFS = sorted(
    [(i, j) for i in range(NZ) for j in range(2) if (i, j) != (0, 0)],
    key=lambda o: -min(o[0], NZ - o[0]),
)


def kernel(
    left_ref, right_ref, lgrad_ref, rgrad_ref, loss_ref,
    lin, rin, lg, rg, lall, rall, er, ec, w, rm_s, rl_s, cm_s, cs_s, rp, ap,
    row_stat, col_stat, bs, br, ls, lr, sib_s, sib_r, zs, zr, zm, part_a, part_b,
    s_in, s_l, r_l, r_sib, s_r, r_r, r_far, s_row, r_row, s_col, r_col,
    s_gb, r_gb, s_gl, r_gl, s_gs, r_gs, s_gz, r_gz, r_gm, s_pa, r_pa, s_pb, r_pb,
):
    me = lax.axis_index("dp")
    core = me % 2
    x = (me // 2) % NA
    y = (me // (2 * NA)) % NA
    z = me // (2 * G)
    a = y * (1 - core) + x * core
    b = x * (1 - core) + y * core
    step_a = 8 - 6 * core
    step_b = 2 + 6 * core
    p = a * NA + b
    mine = 3 * NA + b
    q = z * 2 + core
    here = 3 * 2 + core
    other = 1 - core
    sg = 1 - 2 * core
    scale = 2.0 / math.sqrt(D) * LOG2E

    def plane_dev(pa, pb):
        return (z * (2 * G) + pa * step_a + pb * step_b + core,)

    def line_dev(pz, pc):
        return (pz * (2 * G) + (y * NA + x) * 2 + pc,)

    def zz(d):
        return (z + d + NZ) % NZ

    def chip(d):
        return (d + 3 + NZ) % NZ


    def copy(src, dst, send, recv, dev):
        return pltpu.make_async_remote_copy(
            src_ref=src, dst_ref=dst, send_sem=send, recv_sem=recv, device_id=dev, device_id_type=MESH
        )

    def go(src, dst, send, recv, dev):
        copy(src, dst, send, recv, dev).start()

    def sent(like, send):
        copy(like, like, send, send, line_dev(z, other)).wait_send()

    def received(like, recv):
        copy(like, like, recv, recv, line_dev(z, other)).wait_recv()

    c_left = pltpu.make_async_copy(left_ref, lin, s_in.at[0])
    c_right = pltpu.make_async_copy(right_ref, rin, s_in.at[1])
    c_left.start()
    c_right.start()
    barrier = pltpu.get_barrier_semaphore()
    firsts = [plane_dev((a + d) % NA, b) for d in A_OFFS] + [plane_dev(a, (b + d) % NA) for d in A_OFFS]
    firsts += [line_dev(zz(d), core) for d in (2, -2, 1, -1)] + [line_dev(z, other)]
    for dev in firsts:
        pl.semaphore_signal(barrier, inc=1, device_id=dev, device_id_type=MESH)
    c_left.wait()
    c_right.wait()
    lbf = lin[...].astype(jnp.bfloat16)
    rbf = rin[...].astype(jnp.bfloat16)
    lg[here] = lbf
    rg[mine] = rbf
    matched = jnp.sum(lbf.astype(jnp.float32) * rbf.astype(jnp.float32)) * scale
    pl.semaphore_wait(barrier, len(firsts))

    def line_slot(d, c):
        return lg.at[chip(d) * 2 + c]

    def line_wait(d):
        received(lg.at[here], r_l.at[chip(d)])

    def line_send(of, d):
        go(line_slot(of, core), line_slot(of - d, core), s_l, r_l.at[chip(of - d)], line_dev(zz(d), core))

    def to_sibling(d):
        piece = line_slot(d, core)
        go(piece, piece, s_l, r_sib.at[chip(d)], line_dev(z, other))

    def plane_send(kb, d):
        src = rg.at[3 * NA + kb]
        there = PLACE[-d % NA] * NA + kb
        go(src, rg.at[there], s_r, r_far, plane_dev((a + d) % NA, b))

    for i, d in enumerate((2, -2, 1, -1)):
        line_send(0, d)
    for i, d in enumerate(A_OFFS):
        go(rg.at[mine], rg.at[mine], s_r, r_r.at[b], plane_dev(a, (b + d) % NA))
    for i, d in enumerate(A_OFFS):
        plane_send(b, d)
    to_sibling(0)
    for n, db in enumerate((1, 3, 2)):
        kb = (b + db) % NA
        received(rg.at[mine], r_r.at[kb])
        for i, d in enumerate(A_OFFS):
            plane_send(kb, d)
    line_wait(-2 * sg)
    line_send(-2 * sg, 2 * sg)
    line_send(-2 * sg, sg)
    line_wait(2 * sg)
    line_send(2 * sg, -sg)
    to_sibling(-2 * sg)
    to_sibling(2 * sg)
    for d in (1, -1, 3 * sg, -3 * sg, 4):
        line_wait(d)
        to_sibling(d)
    received(rg.at[pl.ds(0, 12)], r_far)

    def join(src, k, dst):
        two = [src[k].astype(jnp.float32), src[k + 1].astype(jnp.float32)]
        dst[k * ROWS : (k + 2) * ROWS, :] = jnp.concatenate(two, axis=0).astype(jnp.bfloat16)

    for k in range(0, G, 2):
        join(rg, k, rall)

    for t in NEAR_FIRST:
        for k in (2 * t, 2 * t + 1):
            received(lg.at[here], r_sib.at[k])
            join(lg, 2 * k, lall)
        at = slice(t * TM, (t + 1) * TM)
        s = lax.dot_general(
            lall[at, :], rall[...], (((1,), (1,)), ((), ())), preferred_element_type=jnp.float32
        ) * scale
        rm = jnp.max(s, axis=1, keepdims=True)
        e = jnp.exp2(s - rm)
        er[at, :] = e
        rm_s[at, :] = jnp.broadcast_to(rm, (TM, 128))
        rl_s[at, :] = jnp.broadcast_to(rm + jnp.log2(jnp.sum(e, axis=1, keepdims=True)), (TM, 128))
        cm = jnp.max(s, axis=0, keepdims=True)
        e = jnp.exp2(s - cm)
        ec[at, :] = e
        cm_s[t] = cm
        cs_s[t] = jnp.sum(e, axis=0, keepdims=True)

    cm = jnp.max(cm_s[...], axis=0)
    cs = jnp.sum(cs_s[...] * jnp.exp2(cm_s[...] - cm[None]), axis=0)
    col_stat[b, :, 0:B] = cm + jnp.log2(cs)
    col_stat[b, :, B : B + 128] = jnp.full((1, 128), matched, jnp.float32)
    rl = jnp.transpose(rl_s[...])[0:1, :]
    for k in range(NZ):
        row_stat[core, k : k + 1, :] = rl[:, k * 2 * ROWS : (k + 1) * 2 * ROWS]

    for i in range(G - 1):
        dz, dc = LINE_OFFS[i]
        dev = line_dev((z + dz) % NZ, (core + dc) % 2)
        there = (-dz % NZ) * 2 + core
        go(row_stat.at[core], row_stat.at[there], s_row, r_row, dev)
        da, db = PLANE_OFFS[i]
        dev = plane_dev((a + da) % NA, (b + db) % NA)
        there = (-da % NA) * NA + b
        go(col_stat.at[b], col_stat.at[there], s_col, r_col, dev)
    sent(rg.at[pl.ds(0, 15)], s_r)
    sent(lg.at[pl.ds(0, 15)], s_l)
    received(row_stat.at[pl.ds(0, 15)], r_row)
    received(col_stat.at[pl.ds(0, 15)], r_col)

    def combine(v):
        top = jnp.max(v, axis=0)
        return top + jnp.log2(jnp.sum(jnp.exp2(v - top[None]), axis=0))

    rows = [combine(row_stat[2 * d : 2 * d + 2]) for d in range(NZ)]
    rows = [v if d == 0 else jnp.concatenate([v[NZ - d :], v[: NZ - d]], axis=0) for d, v in enumerate(rows)]
    rows = combine(jnp.stack(rows))
    row_lse = jnp.concatenate([rows[k : k + 1, :] for k in range(NZ)], axis=1)

    def in_order(d):
        v = combine(col_stat[d * NA : (d + 1) * NA, :, 0:B])
        if d == 0:
            return v
        places = [PLACE[(off - d) % NA] * TM for off in BUNDLES]
        return jnp.concatenate([v[:, at : at + TM] for at in places], axis=1)

    col_lse = combine(jnp.stack([in_order(d) for d in range(NA)]))
    rm_s[...] = jnp.exp2(rm_s[...] - jnp.transpose(jnp.broadcast_to(row_lse, (128, B))))

    pairs = jnp.sum(col_stat[:, :, B : B + 128], axis=0)
    part_a[q] = jnp.sum(col_lse) - 2.0 * pairs
    part_b[p] = jnp.full((1, 128), jnp.sum(row_lse), jnp.float32)

    col_loc = lax.broadcasted_iota(jnp.int32, (1, B), 1) - mine * ROWS
    col_loc = jnp.where((col_loc >= 0) & (col_loc < ROWS), col_loc, -2)

    for i, d in enumerate(A_OFFS):
        go(part_b.at[p], part_b.at[p], s_pb, r_pb.at[0], plane_dev(a, (b + d) % NA))
    go(part_a.at[q], part_a.at[q], s_pa, r_pa.at[0], line_dev(z, other))
    for t in range(CHUNKS):
        at = slice(t * TM, (t + 1) * TM)
        fc = jnp.exp2(cm_s[t] - col_lse)
        row_loc = lax.broadcasted_iota(jnp.int32, (TM, 1), 0) + (t * TM - here * ROWS)
        row_loc = jnp.where((row_loc >= 0) & (row_loc < ROWS), row_loc, -1)
        ww = er[at, :] * rm_s[at, 0:1] + ec[at, :] * fc
        w[at, :] = jnp.where(row_loc == col_loc, ww - 2.0, ww).astype(jnp.bfloat16)

    def right_step(u):
        rp[u * TN : (u + 1) * TN, :] = lax.dot_general(
            w[:, u * TN : (u + 1) * TN], lall[...], (((0,), (0,)), ((), ())), preferred_element_type=jnp.float32
        )
        for k in range(u * TN // ROWS, (u + 1) * TN // ROWS):
            d = BUNDLES[k // NA]
            if d:
                bs[k] = rp[k * ROWS : (k + 1) * ROWS, :].astype(jnp.bfloat16)
                there = PLACE[-d % NA] * NA + k % NA
                go(bs.at[k], br.at[there], s_gb, r_gb.at[k % NA], plane_dev((a + d) % NA, b))

    def left_step(t):
        part = jnp.dot(w[t * TM : (t + 1) * TM, :], rall[...], preferred_element_type=jnp.float32)
        for j in range(2):
            k = 2 * t + j
            lo = part[2 * j * ROWS : (2 * j + 1) * ROWS, :]
            hi = part[(2 * j + 1) * ROWS : (2 * j + 2) * ROWS, :]
            ap[k] = jnp.where(core == 0, lo, hi)
            sib_s[k] = jnp.where(core == 0, hi, lo).astype(jnp.bfloat16)
            go(sib_s.at[k], sib_r.at[k], s_gs, r_gs.at[k], line_dev(z, other))

    def chip_sum(k):
        received(sib_r.at[0], r_gs.at[k])
        return ap[k] + sib_r[k].astype(jnp.float32)

    def mid(i, owner, d):
        zs[i] = chip_sum(chip(owner)).astype(jnp.bfloat16)
        go(zs.at[i], zm.at[i], s_gz, r_gm.at[i], line_dev(zz(d), core))

    def mid_wait(i):
        received(zm.at[i], r_gm.at[i])
        return zm[i].astype(jnp.float32)

    def end(i, d, value):
        zs[i] = value.astype(jnp.bfloat16)
        go(zs.at[i], zr.at[i - 3], s_gz, r_gz.at[i - 3], line_dev(zz(d), core))

    left_step(3)
    right_step(0)
    left_step(0)
    right_step(1)
    mid(0, 4, -2 * sg)
    mid(1, -3 * sg, -sg)
    mid(2, 3 * sg, sg)
    received(part_b.at[pl.ds(0, 3)], r_pb.at[0])
    own = pl.ds(a * NA, NA)
    for i, d in enumerate(A_OFFS):
        dev = plane_dev((a + d) % NA, b)
        go(part_b.at[own], part_b.at[own], s_pb, r_pb.at[1], dev)
    received(part_a.at[q], r_pa.at[0])
    own = pl.ds(z * 2, 2)
    for i, d in enumerate((4, 3, -3, 2, -2, 1, -1)):
        go(part_a.at[own], part_a.at[own], s_pa, r_pa.at[1], line_dev(zz(d), core))
    right_step(2)
    left_step(2)
    left_step(1)
    end(3, 1, chip_sum(chip(1)))
    end(4, -1, chip_sum(chip(-1)))
    plus = chip_sum(chip(2 * sg))
    minus = chip_sum(chip(-2 * sg))
    lgrad_ref[...] = chip_sum(chip(0))
    end(5, 2 * sg, plus + mid_wait(2))
    end(6, -2 * sg, minus + mid_wait(0) + mid_wait(1))
    def right_sum(kb):
        k = 3 * NA + kb
        total = rp[pl.ds(pl.multiple_of(k * ROWS, ROWS), ROWS), :]
        received(bs.at[pl.ds(0, 3)], r_gb.at[kb])
        for k in range(3):
            total += br[k * NA + kb].astype(jnp.float32)
        return total

    for i, d in enumerate(A_OFFS):
        kb = (b + d) % NA
        ls[i] = right_sum(kb).astype(jnp.bfloat16)
        go(ls.at[i], lr.at[b], s_gl, r_gl.at[b], plane_dev(a, kb))
    rgrad_ref[...] = right_sum(b)
    sent(row_stat.at[pl.ds(0, 15)], s_row)
    sent(col_stat.at[pl.ds(0, 15)], s_col)
    sent(sib_s, s_gs)
    sent(bs, s_gb)
    for i, d in enumerate(A_OFFS):
        received(ls.at[i], r_gl.at[(b + d) % NA])
        rgrad_ref[...] += lr[(b + d) % NA].astype(jnp.float32)
    for i in range(4):
        received(zr.at[i], r_gz.at[i])
        lgrad_ref[...] += zr[i].astype(jnp.float32)
    received(part_b.at[pl.ds(0, 12)], r_pb.at[1])
    received(part_a.at[pl.ds(0, 14)], r_pa.at[1])
    loss_ref[...] = (jnp.sum(part_a[...], axis=0) + jnp.sum(part_b[...], axis=0)) * (LN2 / (2.0 * NZ * 2 * B))
    sent(zs, s_gz)
    sent(ls, s_gl)
    sent(part_b.at[pl.ds(0, 15)], s_pb)
    sent(part_a.at[pl.ds(0, 15)], s_pa)


def shards(left, right):
    f32, bf16 = jnp.float32, jnp.bfloat16
    anywhere = pl.BlockSpec(memory_space=pl.ANY)
    vmem = pl.BlockSpec(memory_space=pltpu.VMEM)
    dma = pltpu.SemaphoreType.DMA
    left_grad, right_grad, loss = pl.pallas_call(
        kernel,
        out_shape=(pltpu.VMEM((ROWS, D), f32), pltpu.VMEM((ROWS, D), f32), pltpu.VMEM((1, 128), f32)),
        in_specs=[anywhere, anywhere],
        out_specs=(vmem, vmem, vmem),
        scratch_shapes=[
            pltpu.VMEM((ROWS, D), f32),
            pltpu.VMEM((ROWS, D), f32),
            pltpu.VMEM((G, ROWS, D), bf16),
            pltpu.VMEM((G, ROWS, D), bf16),
            pltpu.VMEM((B, D), bf16),
            pltpu.VMEM((B, D), bf16),
            pltpu.VMEM((B, B), f32),
            pltpu.VMEM((B, B), f32),
            pltpu.VMEM((B, B), bf16),
            pltpu.VMEM((B, 128), f32),
            pltpu.VMEM((B, 128), f32),
            pltpu.VMEM((CHUNKS, 1, B), f32),
            pltpu.VMEM((CHUNKS, 1, B), f32),
            pltpu.VMEM((B, D), f32),
            pltpu.VMEM((NZ, ROWS, D), f32),
            pltpu.VMEM((G, NZ, 2 * ROWS), f32),
            pltpu.VMEM((G, 1, B + 128), f32),
            pltpu.VMEM((12, ROWS, D), bf16),
            pltpu.VMEM((12, ROWS, D), bf16),
            pltpu.VMEM((3, ROWS, D), bf16),
            pltpu.VMEM((NA, ROWS, D), bf16),
            pltpu.VMEM((NZ, ROWS, D), bf16),
            pltpu.VMEM((NZ, ROWS, D), bf16),
            pltpu.VMEM((7, ROWS, D), bf16),
            pltpu.VMEM((4, ROWS, D), bf16),
            pltpu.VMEM((3, ROWS, D), bf16),
            pltpu.VMEM((G, 1, 128), f32),
            pltpu.VMEM((G, 1, 128), f32),
            dma((2,)),
            dma, dma((NZ,)), dma((NZ,)),
            dma, dma((NA,)), dma,
            dma, dma,
            dma, dma,
            dma, dma((NA,)),
            dma, dma((NA,)),
            dma, dma((NZ,)),
            dma, dma((4,)), dma((3,)),
            dma, dma((2,)),
            dma, dma((2,)),
        ],
        compiler_params=pltpu.CompilerParams(
            collective_id=0, has_side_effects=True, vmem_limit_bytes=56 * 2**20
        ),
        cost_estimate=pl.CostEstimate(flops=6 * B * B * D, bytes_accessed=16 * ROWS * D, transcendentals=2 * B * B),
        name="infonce",
    )(left, right)
    return left_grad, right_grad, loss[0, 0]


def solution(mesh):
    return jax.shard_map(
        shards,
        mesh=mesh,
        in_specs=(P("dp", None), P("dp", None)),
        out_specs=(P("dp", None), P("dp", None), P()),
        check_vma=False,
    )
```

```python
import math

import jax
import jax.numpy as jnp
from jax import lax
from jax.experimental import pallas as pl
from jax.experimental.pallas import tpu as pltpu
from jax.sharding import PartitionSpec as P

MESH = pl.DeviceIdType.MESH
NZ = 8
NA = 4
G = 16
ROWS = 72
D = 384
B = G * ROWS
TM = 4 * ROWS
CHUNKS = B // TM
TN = 384
LOG2E = math.log2(math.e)
LN2 = math.log(2.0)

A_OFFS = (2, 1, 3)
BUNDLES = (2, 1, 3, 0)
PLACE = (3, 1, 0, 2)
NEAR_FIRST = (1, 2, 0, 3)
PLANE_OFFS = sorted(
    [(i, j) for i in range(NA) for j in range(NA) if (i, j) != (0, 0)],
    key=lambda o: -(min(o[0], NA - o[0]) + min(o[1], NA - o[1])),
)
LINE_OFFS = sorted(
    [(i, j) for i in range(NZ) for j in range(2) if (i, j) != (0, 0)],
    key=lambda o: -min(o[0], NZ - o[0]),
)


def kernel(
    left_ref, right_ref, out_ref,
    lin, rin, lg, rg, lall, rall, er, ec, w, rm_s, rl_s, cm_s, cs_s, rp, ap,
    row_stat, col_stat, bs, br, ls, lr, sib_s, sib_r, zs, zr, zm, part_a, part_b,
    s_in, s_l, r_l, r_sib, s_r, r_r, r_far, s_row, r_row, s_col, r_col,
    s_gb, r_gb, s_gl, r_gl, s_gs, r_gs, s_gz, r_gz, r_gm, s_pa, r_pa, s_pb, r_pb,
):
    lgrad_ref, rgrad_ref = out_ref.at[pl.ds(0, ROWS)], out_ref.at[pl.ds(ROWS, ROWS)]
    loss_ref = out_ref.at[pl.ds(2 * ROWS, 1), pl.ds(0, 128)]
    me = lax.axis_index("dp")
    core = me % 2
    x = (me // 2) % NA
    y = (me // (2 * NA)) % NA
    z = me // (2 * G)
    a = y * (1 - core) + x * core
    b = x * (1 - core) + y * core
    step_a = 8 - 6 * core
    step_b = 2 + 6 * core
    p = a * NA + b
    mine = 3 * NA + b
    q = z * 2 + core
    here = 3 * 2 + core
    other = 1 - core
    sg = 1 - 2 * core
    scale = 2.0 / math.sqrt(D) * LOG2E

    def plane_dev(pa, pb):
        return (z * (2 * G) + pa * step_a + pb * step_b + core,)

    def line_dev(pz, pc):
        return (pz * (2 * G) + (y * NA + x) * 2 + pc,)

    def zz(d):
        return (z + d + NZ) % NZ

    def chip(d):
        return (d + 3 + NZ) % NZ


    def copy(src, dst, send, recv, dev):
        return pltpu.make_async_remote_copy(
            src_ref=src, dst_ref=dst, send_sem=send, recv_sem=recv, device_id=dev, device_id_type=MESH
        )

    def go(src, dst, send, recv, dev):
        copy(src, dst, send, recv, dev).start()

    def sent(like, send):
        copy(like, like, send, send, line_dev(z, other)).wait_send()

    def received(like, recv):
        copy(like, like, recv, recv, line_dev(z, other)).wait_recv()

    c_left = pltpu.make_async_copy(left_ref, lin, s_in.at[0])
    c_right = pltpu.make_async_copy(right_ref, rin, s_in.at[1])
    c_left.start()
    c_right.start()
    barrier = pltpu.get_barrier_semaphore()
    firsts = [plane_dev((a + d) % NA, b) for d in A_OFFS] + [plane_dev(a, (b + d) % NA) for d in A_OFFS]
    firsts += [line_dev(zz(d), core) for d in (2, -2, 1, -1)] + [line_dev(z, other)]
    for dev in firsts:
        pl.semaphore_signal(barrier, inc=1, device_id=dev, device_id_type=MESH)
    c_left.wait()
    c_right.wait()
    lbf = lin[...].astype(jnp.bfloat16)
    rbf = rin[...].astype(jnp.bfloat16)
    lg[here] = lbf
    rg[mine] = rbf
    matched = jnp.sum(lbf.astype(jnp.float32) * rbf.astype(jnp.float32)) * scale
    pl.semaphore_wait(barrier, len(firsts))

    def line_slot(d, c):
        return lg.at[chip(d) * 2 + c]

    def line_wait(d):
        received(lg.at[here], r_l.at[chip(d)])

    def line_send(of, d):
        go(line_slot(of, core), line_slot(of - d, core), s_l, r_l.at[chip(of - d)], line_dev(zz(d), core))

    def to_sibling(d):
        piece = line_slot(d, core)
        go(piece, piece, s_l, r_sib.at[chip(d)], line_dev(z, other))

    def plane_send(kb, d):
        src = rg.at[3 * NA + kb]
        there = PLACE[-d % NA] * NA + kb
        go(src, rg.at[there], s_r, r_far, plane_dev((a + d) % NA, b))

    for i, d in enumerate((2, -2, 1, -1)):
        line_send(0, d)
    for i, d in enumerate(A_OFFS):
        go(rg.at[mine], rg.at[mine], s_r, r_r.at[b], plane_dev(a, (b + d) % NA))
    for i, d in enumerate(A_OFFS):
        plane_send(b, d)
    to_sibling(0)
    for n, db in enumerate((1, 3, 2)):
        kb = (b + db) % NA
        received(rg.at[mine], r_r.at[kb])
        for i, d in enumerate(A_OFFS):
            plane_send(kb, d)
    line_wait(-2 * sg)
    line_send(-2 * sg, 2 * sg)
    line_send(-2 * sg, sg)
    line_wait(2 * sg)
    line_send(2 * sg, -sg)
    to_sibling(-2 * sg)
    to_sibling(2 * sg)
    for d in (1, -1, 3 * sg, -3 * sg, 4):
        line_wait(d)
        to_sibling(d)
    received(rg.at[pl.ds(0, 12)], r_far)

    def join(src, k, dst):
        two = [src[k].astype(jnp.float32), src[k + 1].astype(jnp.float32)]
        dst[k * ROWS : (k + 2) * ROWS, :] = jnp.concatenate(two, axis=0).astype(jnp.bfloat16)

    for k in range(0, G, 2):
        join(rg, k, rall)

    for t in NEAR_FIRST:
        for k in (2 * t, 2 * t + 1):
            received(lg.at[here], r_sib.at[k])
            join(lg, 2 * k, lall)
        at = slice(t * TM, (t + 1) * TM)
        s = lax.dot_general(
            lall[at, :], rall[...], (((1,), (1,)), ((), ())), preferred_element_type=jnp.float32
        ) * scale
        rm = jnp.max(s, axis=1, keepdims=True)
        e = jnp.exp2(s - rm)
        er[at, :] = e
        rm_s[at, :] = jnp.broadcast_to(rm, (TM, 128))
        rl_s[at, :] = jnp.broadcast_to(rm + jnp.log2(jnp.sum(e, axis=1, keepdims=True)), (TM, 128))
        cm = jnp.max(s, axis=0, keepdims=True)
        e = jnp.exp2(s - cm)
        ec[at, :] = e
        cm_s[t] = cm
        cs_s[t] = jnp.sum(e, axis=0, keepdims=True)

    cm = jnp.max(cm_s[...], axis=0)
    cs = jnp.sum(cs_s[...] * jnp.exp2(cm_s[...] - cm[None]), axis=0)
    col_stat[b, :, 0:B] = cm + jnp.log2(cs)
    col_stat[b, :, B : B + 128] = jnp.full((1, 128), matched, jnp.float32)
    rl = jnp.transpose(rl_s[...])[0:1, :]
    for k in range(NZ):
        row_stat[core, k : k + 1, :] = rl[:, k * 2 * ROWS : (k + 1) * 2 * ROWS]

    for i in range(G - 1):
        dz, dc = LINE_OFFS[i]
        dev = line_dev((z + dz) % NZ, (core + dc) % 2)
        there = (-dz % NZ) * 2 + core
        go(row_stat.at[core], row_stat.at[there], s_row, r_row, dev)
        da, db = PLANE_OFFS[i]
        dev = plane_dev((a + da) % NA, (b + db) % NA)
        there = (-da % NA) * NA + b
        go(col_stat.at[b], col_stat.at[there], s_col, r_col, dev)
    sent(rg.at[pl.ds(0, 15)], s_r)
    sent(lg.at[pl.ds(0, 15)], s_l)
    received(row_stat.at[pl.ds(0, 15)], r_row)
    received(col_stat.at[pl.ds(0, 15)], r_col)

    def combine(v):
        top = jnp.max(v, axis=0)
        return top + jnp.log2(jnp.sum(jnp.exp2(v - top[None]), axis=0))

    rows = [combine(row_stat[2 * d : 2 * d + 2]) for d in range(NZ)]
    rows = [v if d == 0 else jnp.concatenate([v[NZ - d :], v[: NZ - d]], axis=0) for d, v in enumerate(rows)]
    rows = combine(jnp.stack(rows))
    row_lse = jnp.concatenate([rows[k : k + 1, :] for k in range(NZ)], axis=1)

    def in_order(d):
        v = combine(col_stat[d * NA : (d + 1) * NA, :, 0:B])
        if d == 0:
            return v
        places = [PLACE[(off - d) % NA] * TM for off in BUNDLES]
        return jnp.concatenate([v[:, at : at + TM] for at in places], axis=1)

    col_lse = combine(jnp.stack([in_order(d) for d in range(NA)]))
    rm_s[...] = jnp.exp2(rm_s[...] - jnp.transpose(jnp.broadcast_to(row_lse, (128, B))))

    pairs = jnp.sum(col_stat[:, :, B : B + 128], axis=0)
    part_a[q] = jnp.sum(col_lse) - 2.0 * pairs
    part_b[p] = jnp.full((1, 128), jnp.sum(row_lse), jnp.float32)

    col_loc = lax.broadcasted_iota(jnp.int32, (1, B), 1) - mine * ROWS
    col_loc = jnp.where((col_loc >= 0) & (col_loc < ROWS), col_loc, -2)

    for i, d in enumerate(A_OFFS):
        go(part_b.at[p], part_b.at[p], s_pb, r_pb.at[0], plane_dev(a, (b + d) % NA))
    go(part_a.at[q], part_a.at[q], s_pa, r_pa.at[0], line_dev(z, other))
    for t in range(CHUNKS):
        at = slice(t * TM, (t + 1) * TM)
        fc = jnp.exp2(cm_s[t] - col_lse)
        row_loc = lax.broadcasted_iota(jnp.int32, (TM, 1), 0) + (t * TM - here * ROWS)
        row_loc = jnp.where((row_loc >= 0) & (row_loc < ROWS), row_loc, -1)
        ww = er[at, :] * rm_s[at, 0:1] + ec[at, :] * fc
        w[at, :] = jnp.where(row_loc == col_loc, ww - 2.0, ww).astype(jnp.bfloat16)

    def right_step(u):
        rp[u * TN : (u + 1) * TN, :] = lax.dot_general(
            w[:, u * TN : (u + 1) * TN], lall[...], (((0,), (0,)), ((), ())), preferred_element_type=jnp.float32
        )
        for k in range(u * TN // ROWS, (u + 1) * TN // ROWS):
            d = BUNDLES[k // NA]
            if d:
                bs[k] = rp[k * ROWS : (k + 1) * ROWS, :].astype(jnp.bfloat16)
                there = PLACE[-d % NA] * NA + k % NA
                go(bs.at[k], br.at[there], s_gb, r_gb.at[k % NA], plane_dev((a + d) % NA, b))

    def left_step(t):
        part = jnp.dot(w[t * TM : (t + 1) * TM, :], rall[...], preferred_element_type=jnp.float32)
        for j in range(2):
            k = 2 * t + j
            lo = part[2 * j * ROWS : (2 * j + 1) * ROWS, :]
            hi = part[(2 * j + 1) * ROWS : (2 * j + 2) * ROWS, :]
            ap[k] = jnp.where(core == 0, lo, hi)
            sib_s[k] = jnp.where(core == 0, hi, lo).astype(jnp.bfloat16)
            go(sib_s.at[k], sib_r.at[k], s_gs, r_gs.at[k], line_dev(z, other))

    def chip_sum(k):
        received(sib_r.at[0], r_gs.at[k])
        return ap[k] + sib_r[k].astype(jnp.float32)

    def mid(i, owner, d):
        zs[i] = chip_sum(chip(owner)).astype(jnp.bfloat16)
        go(zs.at[i], zm.at[i], s_gz, r_gm.at[i], line_dev(zz(d), core))

    def mid_wait(i):
        received(zm.at[i], r_gm.at[i])
        return zm[i].astype(jnp.float32)

    def end(i, d, value):
        zs[i] = value.astype(jnp.bfloat16)
        go(zs.at[i], zr.at[i - 3], s_gz, r_gz.at[i - 3], line_dev(zz(d), core))

    left_step(3)
    right_step(0)
    left_step(0)
    right_step(1)
    mid(0, 4, -2 * sg)
    mid(1, -3 * sg, -sg)
    mid(2, 3 * sg, sg)
    received(part_b.at[pl.ds(0, 3)], r_pb.at[0])
    own = pl.ds(a * NA, NA)
    for i, d in enumerate(A_OFFS):
        dev = plane_dev((a + d) % NA, b)
        go(part_b.at[own], part_b.at[own], s_pb, r_pb.at[1], dev)
    received(part_a.at[q], r_pa.at[0])
    own = pl.ds(z * 2, 2)
    for i, d in enumerate((4, 3, -3, 2, -2, 1, -1)):
        go(part_a.at[own], part_a.at[own], s_pa, r_pa.at[1], line_dev(zz(d), core))
    right_step(2)
    left_step(2)
    left_step(1)
    end(3, 1, chip_sum(chip(1)))
    end(4, -1, chip_sum(chip(-1)))
    plus = chip_sum(chip(2 * sg))
    minus = chip_sum(chip(-2 * sg))
    lgrad_ref[...] = chip_sum(chip(0))
    end(5, 2 * sg, plus + mid_wait(2))
    end(6, -2 * sg, minus + mid_wait(0) + mid_wait(1))
    def right_sum(kb):
        k = 3 * NA + kb
        total = rp[pl.ds(pl.multiple_of(k * ROWS, ROWS), ROWS), :]
        received(bs.at[pl.ds(0, 3)], r_gb.at[kb])
        for k in range(3):
            total += br[k * NA + kb].astype(jnp.float32)
        return total

    for i, d in enumerate(A_OFFS):
        kb = (b + d) % NA
        ls[i] = right_sum(kb).astype(jnp.bfloat16)
        go(ls.at[i], lr.at[b], s_gl, r_gl.at[b], plane_dev(a, kb))
    rgrad_ref[...] = right_sum(b)
    sent(row_stat.at[pl.ds(0, 15)], s_row)
    sent(col_stat.at[pl.ds(0, 15)], s_col)
    sent(sib_s, s_gs)
    sent(bs, s_gb)
    for i, d in enumerate(A_OFFS):
        received(ls.at[i], r_gl.at[(b + d) % NA])
        rgrad_ref[...] += lr[(b + d) % NA].astype(jnp.float32)
    for i in range(4):
        received(zr.at[i], r_gz.at[i])
        lgrad_ref[...] += zr[i].astype(jnp.float32)
    received(part_b.at[pl.ds(0, 12)], r_pb.at[1])
    received(part_a.at[pl.ds(0, 14)], r_pa.at[1])
    loss_ref[...] = (jnp.sum(part_a[...], axis=0) + jnp.sum(part_b[...], axis=0)) * (LN2 / (2.0 * NZ * 2 * B))
    sent(zs, s_gz)
    sent(ls, s_gl)
    sent(part_b.at[pl.ds(0, 15)], s_pb)
    sent(part_a.at[pl.ds(0, 15)], s_pa)


def shards(left, right):
    f32, bf16 = jnp.float32, jnp.bfloat16
    anywhere = pl.BlockSpec(memory_space=pl.ANY)
    vmem = pl.BlockSpec(memory_space=pltpu.VMEM)
    dma = pltpu.SemaphoreType.DMA
    out = pl.pallas_call(
        kernel,
        out_shape=pltpu.VMEM((2 * ROWS + 8, D), f32),
        in_specs=[anywhere, anywhere],
        out_specs=vmem,
        scratch_shapes=[
            pltpu.VMEM((ROWS, D), f32),
            pltpu.VMEM((ROWS, D), f32),
            pltpu.VMEM((G, ROWS, D), bf16),
            pltpu.VMEM((G, ROWS, D), bf16),
            pltpu.VMEM((B, D), bf16),
            pltpu.VMEM((B, D), bf16),
            pltpu.VMEM((B, B), f32),
            pltpu.VMEM((B, B), f32),
            pltpu.VMEM((B, B), bf16),
            pltpu.VMEM((B, 128), f32),
            pltpu.VMEM((B, 128), f32),
            pltpu.VMEM((CHUNKS, 1, B), f32),
            pltpu.VMEM((CHUNKS, 1, B), f32),
            pltpu.VMEM((B, D), f32),
            pltpu.VMEM((NZ, ROWS, D), f32),
            pltpu.VMEM((G, NZ, 2 * ROWS), f32),
            pltpu.VMEM((G, 1, B + 128), f32),
            pltpu.VMEM((12, ROWS, D), bf16),
            pltpu.VMEM((12, ROWS, D), bf16),
            pltpu.VMEM((3, ROWS, D), bf16),
            pltpu.VMEM((NA, ROWS, D), bf16),
            pltpu.VMEM((NZ, ROWS, D), bf16),
            pltpu.VMEM((NZ, ROWS, D), bf16),
            pltpu.VMEM((7, ROWS, D), bf16),
            pltpu.VMEM((4, ROWS, D), bf16),
            pltpu.VMEM((3, ROWS, D), bf16),
            pltpu.VMEM((G, 1, 128), f32),
            pltpu.VMEM((G, 1, 128), f32),
            dma((2,)),
            dma, dma((NZ,)), dma((NZ,)),
            dma, dma((NA,)), dma,
            dma, dma,
            dma, dma,
            dma, dma((NA,)),
            dma, dma((NA,)),
            dma, dma((NZ,)),
            dma, dma((4,)), dma((3,)),
            dma, dma((2,)),
            dma, dma((2,)),
        ],
        compiler_params=pltpu.CompilerParams(
            collective_id=0, has_side_effects=True, vmem_limit_bytes=56 * 2**20
        ),
        cost_estimate=pl.CostEstimate(flops=6 * B * B * D, bytes_accessed=16 * ROWS * D, transcendentals=2 * B * B),
        name="infonce",
    )(left, right)
    return out[:ROWS], out[ROWS : 2 * ROWS], out[2 * ROWS, 0]


def solution(mesh):
    return jax.shard_map(
        shards,
        mesh=mesh,
        in_specs=(P("dp", None), P("dp", None)),
        out_specs=(P("dp", None), P("dp", None), P()),
        check_vma=False,
    )
```

```python
import math

import jax
import jax.numpy as jnp
from jax import lax
from jax.experimental import pallas as pl
from jax.experimental.pallas import tpu as pltpu
from jax.sharding import PartitionSpec as P

MESH = pl.DeviceIdType.MESH
NZ = 8
NA = 4
G = 16
ROWS = 72
D = 384
B = G * ROWS
TM = 4 * ROWS
CHUNKS = B // TM
TN = 384
LOG2E = math.log2(math.e)
LN2 = math.log(2.0)

A_OFFS = (2, 1, 3)
BUNDLES = (2, 1, 3, 0)
PLACE = (3, 1, 0, 2)
NEAR_FIRST = (1, 2, 0, 3)
PLANE_OFFS = sorted(
    [(i, j) for i in range(NA) for j in range(NA) if (i, j) != (0, 0)],
    key=lambda o: -(min(o[0], NA - o[0]) + min(o[1], NA - o[1])),
)
LINE_OFFS = sorted(
    [(i, j) for i in range(NZ) for j in range(2) if (i, j) != (0, 0)],
    key=lambda o: -min(o[0], NZ - o[0]),
)


def kernel(
    left_ref, right_ref, out_ref,
    lin, rin, lg, rg, lall, rall, er, ec, w, rm_s, rl_s, cm_s, cs_s, rp, ap,
    row_stat, col_stat, bs, br, ls, lr, sib_s, sib_r, zs, zr, zm, part_a, part_b,
    s_in, s_l, r_l, r_sib, s_r, r_r, r_far, s_row, r_row, s_col, r_col,
    s_gb, r_gb, s_gl, r_gl, s_gs, r_gs, s_gz, r_gz, r_gm, s_pa, r_pa, s_pb, r_pb,
):
    lgrad_ref, rgrad_ref = out_ref.at[pl.ds(0, ROWS)], out_ref.at[pl.ds(ROWS, ROWS)]
    loss_ref = out_ref.at[pl.ds(2 * ROWS, 1), pl.ds(0, 128)]
    me = lax.axis_index("dp")
    core = me % 2
    x = (me // 2) % NA
    y = (me // (2 * NA)) % NA
    z = me // (2 * G)
    a = y * (1 - core) + x * core
    b = x * (1 - core) + y * core
    step_a = 8 - 6 * core
    step_b = 2 + 6 * core
    p = a * NA + b
    mine = 3 * NA + b
    q = z * 2 + core
    here = 3 * 2 + core
    other = 1 - core
    sg = 1 - 2 * core
    scale = 2.0 / math.sqrt(D) * LOG2E

    def plane_dev(pa, pb):
        return (z * (2 * G) + pa * step_a + pb * step_b + core,)

    def line_dev(pz, pc):
        return (pz * (2 * G) + (y * NA + x) * 2 + pc,)

    def zz(d):
        return (z + d + NZ) % NZ

    def chip(d):
        return (d + 3 + NZ) % NZ


    def copy(src, dst, send, recv, dev):
        return pltpu.make_async_remote_copy(
            src_ref=src, dst_ref=dst, send_sem=send, recv_sem=recv, device_id=dev, device_id_type=MESH
        )

    def go(src, dst, send, recv, dev):
        copy(src, dst, send, recv, dev).start()

    def sent(like, send):
        copy(like, like, send, send, line_dev(z, other)).wait_send()

    def received(like, recv):
        copy(like, like, recv, recv, line_dev(z, other)).wait_recv()

    c_left = pltpu.make_async_copy(left_ref, lin, s_in.at[0])
    c_right = pltpu.make_async_copy(right_ref, rin, s_in.at[1])
    barrier = pltpu.get_barrier_semaphore()
    firsts = [plane_dev((a + d) % NA, b) for d in A_OFFS] + [plane_dev(a, (b + d) % NA) for d in A_OFFS]
    firsts += [line_dev(zz(d), core) for d in (2, -2, 1, -1)] + [line_dev(z, other)]
    for dev in firsts:
        pl.semaphore_signal(barrier, inc=1, device_id=dev, device_id_type=MESH)
    c_left.start()
    c_right.start()
    c_left.wait()
    c_right.wait()
    lbf = lin[...].astype(jnp.bfloat16)
    rbf = rin[...].astype(jnp.bfloat16)
    lg[here] = lbf
    rg[mine] = rbf
    pl.semaphore_wait(barrier, len(firsts))

    def line_slot(d, c):
        return lg.at[chip(d) * 2 + c]

    def line_wait(d):
        received(lg.at[here], r_l.at[chip(d)])

    def line_send(of, d):
        go(line_slot(of, core), line_slot(of - d, core), s_l, r_l.at[chip(of - d)], line_dev(zz(d), core))

    def to_sibling(d):
        piece = line_slot(d, core)
        go(piece, piece, s_l, r_sib.at[chip(d)], line_dev(z, other))

    def plane_send(kb, d):
        src = rg.at[3 * NA + kb]
        there = PLACE[-d % NA] * NA + kb
        go(src, rg.at[there], s_r, r_far, plane_dev((a + d) % NA, b))

    for i, d in enumerate((2, -2, 1, -1)):
        line_send(0, d)
    for i, d in enumerate(A_OFFS):
        go(rg.at[mine], rg.at[mine], s_r, r_r.at[b], plane_dev(a, (b + d) % NA))
    for i, d in enumerate(A_OFFS):
        plane_send(b, d)
    to_sibling(0)
    matched = jnp.sum(lbf.astype(jnp.float32) * rbf.astype(jnp.float32)) * scale
    for n, db in enumerate((1, 3, 2)):
        kb = (b + db) % NA
        received(rg.at[mine], r_r.at[kb])
        for i, d in enumerate(A_OFFS):
            plane_send(kb, d)
    line_wait(-2 * sg)
    line_send(-2 * sg, 2 * sg)
    line_send(-2 * sg, sg)
    line_wait(2 * sg)
    line_send(2 * sg, -sg)
    to_sibling(-2 * sg)
    to_sibling(2 * sg)
    for d in (1, -1, 3 * sg, -3 * sg, 4):
        line_wait(d)
        to_sibling(d)
    received(rg.at[pl.ds(0, 12)], r_far)

    def join(src, k, dst):
        two = [src[k].astype(jnp.float32), src[k + 1].astype(jnp.float32)]
        dst[k * ROWS : (k + 2) * ROWS, :] = jnp.concatenate(two, axis=0).astype(jnp.bfloat16)

    for k in range(0, G, 2):
        join(rg, k, rall)

    for t in NEAR_FIRST:
        for k in (2 * t, 2 * t + 1):
            received(lg.at[here], r_sib.at[k])
            join(lg, 2 * k, lall)
        at = slice(t * TM, (t + 1) * TM)
        s = lax.dot_general(
            lall[at, :], rall[...], (((1,), (1,)), ((), ())), preferred_element_type=jnp.float32
        ) * scale
        rm = jnp.max(s, axis=1, keepdims=True)
        e = jnp.exp2(s - rm)
        er[at, :] = e
        rm_s[at, :] = jnp.broadcast_to(rm, (TM, 128))
        rl_s[at, :] = jnp.broadcast_to(rm + jnp.log2(jnp.sum(e, axis=1, keepdims=True)), (TM, 128))
        cm = jnp.max(s, axis=0, keepdims=True)
        e = jnp.exp2(s - cm)
        ec[at, :] = e
        cm_s[t] = cm
        cs_s[t] = jnp.sum(e, axis=0, keepdims=True)

    cm = jnp.max(cm_s[...], axis=0)
    cs = jnp.sum(cs_s[...] * jnp.exp2(cm_s[...] - cm[None]), axis=0)
    col_stat[b, :, 0:B] = cm + jnp.log2(cs)
    col_stat[b, :, B : B + 128] = jnp.full((1, 128), matched, jnp.float32)
    rl = jnp.transpose(rl_s[...])[0:1, :]
    for k in range(NZ):
        row_stat[core, k : k + 1, :] = rl[:, k * 2 * ROWS : (k + 1) * 2 * ROWS]

    for i in range(G - 1):
        dz, dc = LINE_OFFS[i]
        dev = line_dev((z + dz) % NZ, (core + dc) % 2)
        there = (-dz % NZ) * 2 + core
        go(row_stat.at[core], row_stat.at[there], s_row, r_row, dev)
        da, db = PLANE_OFFS[i]
        dev = plane_dev((a + da) % NA, (b + db) % NA)
        there = (-da % NA) * NA + b
        go(col_stat.at[b], col_stat.at[there], s_col, r_col, dev)
    sent(rg.at[pl.ds(0, 15)], s_r)
    sent(lg.at[pl.ds(0, 15)], s_l)
    received(row_stat.at[pl.ds(0, 15)], r_row)
    received(col_stat.at[pl.ds(0, 15)], r_col)

    def combine(v):
        top = jnp.max(v, axis=0)
        return top + jnp.log2(jnp.sum(jnp.exp2(v - top[None]), axis=0))

    rows = [combine(row_stat[2 * d : 2 * d + 2]) for d in range(NZ)]
    rows = [v if d == 0 else jnp.concatenate([v[NZ - d :], v[: NZ - d]], axis=0) for d, v in enumerate(rows)]
    rows = combine(jnp.stack(rows))
    row_lse = jnp.concatenate([rows[k : k + 1, :] for k in range(NZ)], axis=1)

    def in_order(d):
        v = combine(col_stat[d * NA : (d + 1) * NA, :, 0:B])
        if d == 0:
            return v
        places = [PLACE[(off - d) % NA] * TM for off in BUNDLES]
        return jnp.concatenate([v[:, at : at + TM] for at in places], axis=1)

    col_lse = combine(jnp.stack([in_order(d) for d in range(NA)]))
    rm_s[...] = jnp.exp2(rm_s[...] - jnp.transpose(jnp.broadcast_to(row_lse, (128, B))))

    pairs = jnp.sum(col_stat[:, :, B : B + 128], axis=0)
    part_a[q] = jnp.sum(col_lse) - 2.0 * pairs
    part_b[p] = jnp.full((1, 128), jnp.sum(row_lse), jnp.float32)

    col_loc = lax.broadcasted_iota(jnp.int32, (1, B), 1) - mine * ROWS
    col_loc = jnp.where((col_loc >= 0) & (col_loc < ROWS), col_loc, -2)

    for i, d in enumerate(A_OFFS):
        go(part_b.at[p], part_b.at[p], s_pb, r_pb.at[0], plane_dev(a, (b + d) % NA))
    go(part_a.at[q], part_a.at[q], s_pa, r_pa.at[0], line_dev(z, other))
    for t in range(CHUNKS):
        at = slice(t * TM, (t + 1) * TM)
        fc = jnp.exp2(cm_s[t] - col_lse)
        row_loc = lax.broadcasted_iota(jnp.int32, (TM, 1), 0) + (t * TM - here * ROWS)
        row_loc = jnp.where((row_loc >= 0) & (row_loc < ROWS), row_loc, -1)
        ww = er[at, :] * rm_s[at, 0:1] + ec[at, :] * fc
        w[at, :] = jnp.where(row_loc == col_loc, ww - 2.0, ww).astype(jnp.bfloat16)

    def right_step(u):
        rp[u * TN : (u + 1) * TN, :] = lax.dot_general(
            w[:, u * TN : (u + 1) * TN], lall[...], (((0,), (0,)), ((), ())), preferred_element_type=jnp.float32
        )
        for k in range(u * TN // ROWS, (u + 1) * TN // ROWS):
            d = BUNDLES[k // NA]
            if d:
                bs[k] = rp[k * ROWS : (k + 1) * ROWS, :].astype(jnp.bfloat16)
                there = PLACE[-d % NA] * NA + k % NA
                go(bs.at[k], br.at[there], s_gb, r_gb.at[k % NA], plane_dev((a + d) % NA, b))

    def left_step(t):
        part = jnp.dot(w[t * TM : (t + 1) * TM, :], rall[...], preferred_element_type=jnp.float32)
        for j in range(2):
            k = 2 * t + j
            lo = part[2 * j * ROWS : (2 * j + 1) * ROWS, :]
            hi = part[(2 * j + 1) * ROWS : (2 * j + 2) * ROWS, :]
            ap[k] = jnp.where(core == 0, lo, hi)
            sib_s[k] = jnp.where(core == 0, hi, lo).astype(jnp.bfloat16)
            go(sib_s.at[k], sib_r.at[k], s_gs, r_gs.at[k], line_dev(z, other))

    def chip_sum(k):
        received(sib_r.at[0], r_gs.at[k])
        return ap[k] + sib_r[k].astype(jnp.float32)

    def mid(i, owner, d):
        zs[i] = chip_sum(chip(owner)).astype(jnp.bfloat16)
        go(zs.at[i], zm.at[i], s_gz, r_gm.at[i], line_dev(zz(d), core))

    def mid_wait(i):
        received(zm.at[i], r_gm.at[i])
        return zm[i].astype(jnp.float32)

    def end(i, d, value):
        zs[i] = value.astype(jnp.bfloat16)
        go(zs.at[i], zr.at[i - 3], s_gz, r_gz.at[i - 3], line_dev(zz(d), core))

    left_step(3)
    right_step(0)
    left_step(0)
    right_step(1)
    mid(0, 4, -2 * sg)
    mid(1, -3 * sg, -sg)
    mid(2, 3 * sg, sg)
    received(part_b.at[pl.ds(0, 3)], r_pb.at[0])
    own = pl.ds(a * NA, NA)
    for i, d in enumerate(A_OFFS):
        dev = plane_dev((a + d) % NA, b)
        go(part_b.at[own], part_b.at[own], s_pb, r_pb.at[1], dev)
    received(part_a.at[q], r_pa.at[0])
    own = pl.ds(z * 2, 2)
    for i, d in enumerate((4, 3, -3, 2, -2, 1, -1)):
        go(part_a.at[own], part_a.at[own], s_pa, r_pa.at[1], line_dev(zz(d), core))
    right_step(2)
    left_step(2)
    left_step(1)
    end(3, 1, chip_sum(chip(1)))
    end(4, -1, chip_sum(chip(-1)))
    plus = chip_sum(chip(2 * sg))
    minus = chip_sum(chip(-2 * sg))
    lgrad_ref[...] = chip_sum(chip(0))
    end(5, 2 * sg, plus + mid_wait(2))
    end(6, -2 * sg, minus + mid_wait(0) + mid_wait(1))
    def right_sum(kb):
        k = 3 * NA + kb
        total = rp[pl.ds(pl.multiple_of(k * ROWS, ROWS), ROWS), :]
        received(bs.at[pl.ds(0, 3)], r_gb.at[kb])
        for k in range(3):
            total += br[k * NA + kb].astype(jnp.float32)
        return total

    for i, d in enumerate(A_OFFS):
        kb = (b + d) % NA
        ls[i] = right_sum(kb).astype(jnp.bfloat16)
        go(ls.at[i], lr.at[b], s_gl, r_gl.at[b], plane_dev(a, kb))
    rgrad_ref[...] = right_sum(b)
    sent(row_stat.at[pl.ds(0, 15)], s_row)
    sent(col_stat.at[pl.ds(0, 15)], s_col)
    sent(sib_s, s_gs)
    sent(bs, s_gb)
    for i, d in enumerate(A_OFFS):
        received(ls.at[i], r_gl.at[(b + d) % NA])
        rgrad_ref[...] += lr[(b + d) % NA].astype(jnp.float32)
    for i in range(4):
        received(zr.at[i], r_gz.at[i])
        lgrad_ref[...] += zr[i].astype(jnp.float32)
    received(part_b.at[pl.ds(0, 12)], r_pb.at[1])
    received(part_a.at[pl.ds(0, 14)], r_pa.at[1])
    loss_ref[...] = (jnp.sum(part_a[...], axis=0) + jnp.sum(part_b[...], axis=0)) * (LN2 / (2.0 * NZ * 2 * B))
    sent(zs, s_gz)
    sent(ls, s_gl)
    sent(part_b.at[pl.ds(0, 15)], s_pb)
    sent(part_a.at[pl.ds(0, 15)], s_pa)


def shards(left, right):
    f32, bf16 = jnp.float32, jnp.bfloat16
    anywhere = pl.BlockSpec(memory_space=pl.ANY)
    vmem = pl.BlockSpec(memory_space=pltpu.VMEM)
    dma = pltpu.SemaphoreType.DMA
    out = pl.pallas_call(
        kernel,
        out_shape=pltpu.VMEM((2 * ROWS + 8, D), f32),
        in_specs=[anywhere, anywhere],
        out_specs=vmem,
        scratch_shapes=[
            pltpu.VMEM((ROWS, D), f32),
            pltpu.VMEM((ROWS, D), f32),
            pltpu.VMEM((G, ROWS, D), bf16),
            pltpu.VMEM((G, ROWS, D), bf16),
            pltpu.VMEM((B, D), bf16),
            pltpu.VMEM((B, D), bf16),
            pltpu.VMEM((B, B), f32),
            pltpu.VMEM((B, B), f32),
            pltpu.VMEM((B, B), bf16),
            pltpu.VMEM((B, 128), f32),
            pltpu.VMEM((B, 128), f32),
            pltpu.VMEM((CHUNKS, 1, B), f32),
            pltpu.VMEM((CHUNKS, 1, B), f32),
            pltpu.VMEM((B, D), f32),
            pltpu.VMEM((NZ, ROWS, D), f32),
            pltpu.VMEM((G, NZ, 2 * ROWS), f32),
            pltpu.VMEM((G, 1, B + 128), f32),
            pltpu.VMEM((12, ROWS, D), bf16),
            pltpu.VMEM((12, ROWS, D), bf16),
            pltpu.VMEM((3, ROWS, D), bf16),
            pltpu.VMEM((NA, ROWS, D), bf16),
            pltpu.VMEM((NZ, ROWS, D), bf16),
            pltpu.VMEM((NZ, ROWS, D), bf16),
            pltpu.VMEM((7, ROWS, D), bf16),
            pltpu.VMEM((4, ROWS, D), bf16),
            pltpu.VMEM((3, ROWS, D), bf16),
            pltpu.VMEM((G, 1, 128), f32),
            pltpu.VMEM((G, 1, 128), f32),
            dma((2,)),
            dma, dma((NZ,)), dma((NZ,)),
            dma, dma((NA,)), dma,
            dma, dma,
            dma, dma,
            dma, dma((NA,)),
            dma, dma((NA,)),
            dma, dma((NZ,)),
            dma, dma((4,)), dma((3,)),
            dma, dma((2,)),
            dma, dma((2,)),
        ],
        compiler_params=pltpu.CompilerParams(
            collective_id=0, has_side_effects=True, vmem_limit_bytes=56 * 2**20
        ),
        cost_estimate=pl.CostEstimate(flops=6 * B * B * D, bytes_accessed=16 * ROWS * D, transcendentals=2 * B * B),
        name="infonce",
    )(left, right)
    return out[:ROWS], out[ROWS : 2 * ROWS], out[2 * ROWS, 0]


def solution(mesh):
    return jax.shard_map(
        shards,
        mesh=mesh,
        in_specs=(P("dp", None), P("dp", None)),
        out_specs=(P("dp", None), P("dp", None), P()),
        check_vma=False,
    )
```
